512 devices in a mesh: frames: 128 (over z, y, core), heads: 4 (over x).
Axes of the slice: x: 4, y: 4, z: 16, core: 2. Of those that a mesh axis runs over, the one named last changes fastest.
Arguments:
- queries: bfloat16 [32768, 1536], P(('frames', 'heads')), may hold values from -6 to 6
- keys: bfloat16 [32768, 1536], P(('frames', 'heads')), may hold values from -12 to 12
- values: bfloat16 [32768, 1536], P(('frames', 'heads')), may hold values from -24 to 24
- block_picks: int32 [128, 128, 2], replicated, may hold values from 0 to 1, as said below
- block_counts: int32 [128, 128], replicated, may hold values from 0 to 2, as said below
Outputs:
- attended: bfloat16 [32768, 1536], P(('frames', 'heads'))
The draws below stay inside these ranges and needn't reach their ends.
Inputs may be any that keep to these rules, and one draw needn't show every extreme that they name: block_picks[g, h, :] are 2 distinct block numbers. block_counts[g, h] is 2 where |g - h| = 1, and 0 where |g - h| is not a power of two.
All inputs are finite; a program needn't handle non-finite values.
Results may differ from the reference program's by a relative error of at most 0.0065.
Values may be sent and summed in bfloat16 or wider, within the bound.
A program may use at most 64 MiB of HBM per device.

```python
import math
import jax
import jax.numpy as jnp
from jax import lax

HEADS = 12
HEAD_DIM = 128
TOK_DEV = 64
BLOCK = 128
PICK = 2
WIDTH = 1536
GROUPS = 128
NB = 2
TOKENS = 32768
N_HEADS = 4


def draw_queries(key, part):
    key = jax.random.fold_in(key, 5)
    base = jnp.clip(jax.random.normal(key, (TOKENS, WIDTH), jnp.float32), -6.0, 6.0)
    return base.astype(jnp.bfloat16)


def draw_keys(key, part):
    key = jax.random.fold_in(key, 7)
    base = jnp.clip(2.0 * jax.random.normal(key, (TOKENS, WIDTH), jnp.float32), -12.0, 12.0)
    return base.astype(jnp.bfloat16)


def draw_block_picks(key, part):
    key = jax.random.fold_in(key, 21)
    row_keys = jax.random.split(key, GROUPS * GROUPS)
    chosen = jax.vmap(lambda one_key: jax.random.permutation(one_key, NB)[:PICK])(row_keys)
    return chosen.reshape(GROUPS, GROUPS, PICK).astype(jnp.int32)


def draw_block_counts(key, part):
    key = jax.random.fold_in(key, 33)
    rows_index = jnp.arange(GROUPS)[:, None]
    cols_index = jnp.arange(GROUPS)[None, :]
    apart = jnp.abs(rows_index - cols_index)
    doubling = jnp.zeros((GROUPS, GROUPS), dtype=bool)
    for exponent in range(GROUPS.bit_length()):
        doubling = doubling | (apart == 2 ** exponent)
    drawn = jax.random.randint(key, (GROUPS, GROUPS), 0, PICK + 1)
    return jnp.where(apart == 1, PICK, jnp.where(doubling, drawn, 0)).astype(jnp.int32)


def steps_of(rng, extent, cuts, smallest, top_value):
    loudness = 1.0
    for position, blocks in cuts:
        heights = jax.random.uniform(jax.random.fold_in(jax.random.fold_in(rng, 6), position), (blocks,), jnp.float32, smallest / len(cuts), top_value / len(cuts))
        loudness = loudness * jnp.repeat(jnp.exp(heights), extent[position] // blocks).reshape((-1,) + (1,) * (len(extent) - 1 - position))
    return loudness


def gaussian(key, dims, deviation, most, cuts=(), held_as=jnp.bfloat16):
    values = deviation * jax.random.normal(key, dims, jnp.float32)
    if cuts:
        values = values * steps_of(key, dims, cuts, -0.22, 0.18)
    return jnp.clip(values, -most, most).astype(held_as)


def setup_inputs(seed: int = 0) -> dict:
    seeds = jax.random.split(jax.random.key(seed), 6)
    queries = draw_queries(jax.random.fold_in(seeds[5], 71), 0)
    keys = draw_keys(jax.random.fold_in(seeds[5], 71), 0)
    values = gaussian(seeds[2], (TOKENS, WIDTH), 4.0, 24.0, ((0, 512),))
    block_picks = draw_block_picks(jax.random.fold_in(seeds[5], 71), 0)
    block_counts = draw_block_counts(jax.random.fold_in(seeds[5], 71), 0)
    return {"queries": queries, "keys": keys, "values": values, "block_picks": block_picks, "block_counts": block_counts}


def reference(queries, keys, values, block_picks, block_counts):
    group_len = TOK_DEV * N_HEADS
    block_count = group_len // BLOCK
    query_groups = queries.reshape(GROUPS, group_len, HEADS, HEAD_DIM)
    key_groups = keys.reshape(GROUPS, group_len, HEADS, HEAD_DIM)
    value_groups = values.reshape(GROUPS, group_len, HEADS, HEAD_DIM)
    offsets = []
    for exponent in range(GROUPS.bit_length()):
        if 2 ** exponent < GROUPS:
            offsets.append(2 ** exponent)
            offsets.append(-2 ** exponent)
    slot_block = jnp.arange(PICK * BLOCK, dtype=jnp.int32) // BLOCK

    def one_group(own_group):
        key_parts = [key_groups[own_group]]
        value_parts = [value_groups[own_group]]
        mask_parts = [jnp.ones((group_len,), dtype=bool)]
        for offset in offsets:
            source = own_group - offset
            inside = (source >= 0) & (source < GROUPS)
            source_row = jnp.clip(source, 0, GROUPS - 1).astype(jnp.int32)
            chosen = block_picks[own_group, source_row].astype(jnp.int32)
            far_keys = key_groups[source_row].reshape(block_count, BLOCK, HEADS, HEAD_DIM)
            far_values = value_groups[source_row].reshape(block_count, BLOCK, HEADS, HEAD_DIM)
            key_parts.append(jnp.take(far_keys, chosen, axis=0).reshape(PICK * BLOCK, HEADS, HEAD_DIM))
            value_parts.append(jnp.take(far_values, chosen, axis=0).reshape(PICK * BLOCK, HEADS, HEAD_DIM))
            live_count = jnp.where(inside, block_counts[own_group, source_row], 0)
            mask_parts.append(slot_block < live_count)
        all_keys = jnp.concatenate(key_parts, axis=0)
        all_values = jnp.concatenate(value_parts, axis=0)
        live_mask = jnp.concatenate(mask_parts, axis=0)
        scores = jnp.einsum('qhd,khd->hqk', query_groups[own_group].astype(jnp.float32), all_keys.astype(jnp.float32)) / math.sqrt(HEAD_DIM)
        masked = jnp.where(live_mask[None, None, :], scores, -jnp.inf)
        maximum = lax.optimization_barrier(jnp.max(masked, axis=2))
        weights = jnp.exp(masked - maximum[:, :, None])
        row_total = lax.optimization_barrier(jnp.sum(weights, axis=2))
        rounded = lax.optimization_barrier(weights.astype(jnp.bfloat16)).astype(jnp.float32)
        mixed = jnp.einsum('hqk,khd->qhd', rounded, all_values.astype(jnp.float32))
        mixed = mixed / jnp.transpose(row_total)[:, :, None]
        return mixed.reshape(group_len, HEADS * HEAD_DIM).astype(jnp.bfloat16)
    result = lax.map(one_group, jnp.arange(GROUPS, dtype=jnp.int32))
    return result.reshape(TOKENS, HEADS * HEAD_DIM)
```

```python
import functools
import math

import jax
import jax.numpy as jnp
from jax import lax
from jax.experimental import pallas as pl
from jax.experimental.pallas import tpu as pltpu
from jax.sharding import PartitionSpec as P

MESH = pl.DeviceIdType.MESH

NZ, NY, NC, NX = 16, 4, 2, 4
GROUPS = NZ * NY * NC
HEADS = 3
DIM = 128
BLOCK = 128
TOK = 64
ROWS = TOK * NX
HIDE = 1e30
EXPONENT = math.log2(math.e) / math.sqrt(DIM)

OWN = 0
BELOW = 0
ABOVE = 4
M2, P2, M4, P4, SIB, SIB2, VIA_M4, VIA_P4 = 9, 10, 11, 12, 13, 14, 15, 16
SLOTS = 17


def kernel(
    q_hbm, k_hbm, v_hbm, picks_hbm, counts_hbm, out_hbm,
    kv, far, qs, os, acc, top, total, counts, picks,
    in_send, in_recv, in_local, kv_send, kv_recv, long_send, long_recv, short_send, short_recv,
    out_send, out_recv, out_local, small_sem,
):
    me = lax.axis_index("frames")
    mx = lax.axis_index("heads")
    core = lax.rem(me, NC)
    my = lax.rem(me // NC, NY)
    mz = me // (NC * NY)

    def frame(z, y, c):
        return (z * NY + y) * NC + c

    up = (frame(lax.rem(mz + 1, NZ), my, core), mx)
    down = (frame(lax.rem(mz + NZ - 1, NZ), my, core), mx)
    right = (frame(mz, lax.rem(my + 1, NY), core), mx)
    left = (frame(mz, lax.rem(my + NY - 1, NY), core), mx)
    sibling = (frame(mz, my, 1 - core), mx)
    others = [(me, lax.rem(mx + d, NX)) for d in (1, 2, 3)]

    table = [
        pltpu.make_async_copy(counts_hbm.at[pl.ds(me, 1)], counts, small_sem.at[0]),
        pltpu.make_async_copy(picks_hbm.at[me], picks, small_sem.at[1]),
    ]
    for copy in table:
        copy.start()

    barrier = pltpu.get_barrier_semaphore()
    partners = [up, down, right, left, sibling] + others
    for partner in partners:
        pl.semaphore_signal(barrier, inc=1, device_id=partner, device_id_type=MESH)
    pl.semaphore_wait(barrier, len(partners))

    def landing(t, h, x):
        rows = pl.ds(pl.multiple_of(x * TOK, TOK), TOK)
        if t == 2:
            return qs.at[h, rows, :]
        return kv.at[OWN, h, t, rows, :]

    def piece(t, h, x):
        source = (k_hbm, v_hbm, q_hbm)[t]
        return source.at[:, pl.ds(pl.multiple_of((x * HEADS + h) * DIM, DIM), DIM)]

    def exchange(t, h, d):
        target = lax.rem(mx + d, NX)
        return pltpu.make_async_remote_copy(
            src_ref=piece(t, h, target),
            dst_ref=landing(t, h, mx),
            send_sem=in_send.at[t, h, d - 1],
            recv_sem=in_recv.at[t, h, d - 1],
            device_id=(me, target),
            device_id_type=MESH,
        )

    def kept(t, h):
        return pltpu.make_async_copy(piece(t, h, mx), landing(t, h, mx), in_local.at[t, h])

    def arrived(t, h):
        kept(t, h).wait()
        for d in (1, 2, 3):
            source = lax.rem(mx + NX - d, NX)
            there = landing(t, h, source)
            pltpu.make_async_copy(there, there, in_recv.at[t, h, d - 1]).wait()

    for h in range(HEADS):
        for t in (0, 1):
            for d in (2, 1, 3):
                exchange(t, h, d).start()
            kept(t, h).start()
    for h in range(HEADS):
        for d in (2, 1, 3):
            exchange(2, h, d).start()
        kept(2, h).start()

    def pass_on(source, slot, h, target):
        return pltpu.make_async_remote_copy(
            src_ref=kv.at[source, h],
            dst_ref=kv.at[slot, h],
            send_sem=kv_send.at[slot - M2, h],
            recv_sem=kv_recv.at[slot - M2, h],
            device_id=target,
            device_id_type=MESH,
        )

    def await_slot(slot, h):
        there = kv.at[slot, h]
        pltpu.make_async_copy(there, there, kv_recv.at[slot - M2, h]).wait()

    ways = (up, down)
    depth = (mz, NZ - 1 - mz)

    def held(way, k, h, t):
        if k == 0:
            return kv.at[OWN, h, t]
        if k <= 4:
            return kv.at[(BELOW, ABOVE)[way] + k, h, t]
        return far.at[k - 5, way, h]

    def pass_along(way, k, h, t, send, recv):
        return pltpu.make_async_remote_copy(
            src_ref=held(way, k - 1, h, t),
            dst_ref=held(way, k, h, t),
            send_sem=send.at[way, k - 1, h],
            recv_sem=recv.at[way, k - 1, h],
            device_id=ways[way],
            device_id_type=MESH,
        )

    def pass_long(way, k, h):
        return pass_along(way, k, h, way, long_send, long_recv)

    def pass_short(way, k, h):
        return pass_along(way, k, h, 1 - way, short_send, short_recv)

    def takes(way, k):
        d = depth[way]
        return ((d >= 3) & (d <= NZ - 2)) if k == 3 else d >= k

    def gives(way, k):
        d = depth[way]
        return ((d >= 2) & (d <= NZ - 3)) if k == 3 else (d >= k - 1) & (d <= NZ - 2)

    def long_hop(k, h):
        for way in (0, 1):
            there = held(way, k, h, way)
            pltpu.make_async_copy(there, there, long_recv.at[way, k - 1, h]).wait()
            if k < 8:
                pass_long(way, k + 1, h).start()

    def short_hop(k, h):
        for way in (0, 1):
            @pl.when(takes(way, k))
            def _():
                there = held(way, k, h, 1 - way)
                pltpu.make_async_copy(there, there, short_recv.at[way, k - 1, h]).wait()

            if k < 4:
                @pl.when(gives(way, k + 1))
                def _():
                    pass_short(way, k + 1, h).start()

    for way in (0, 1):
        for k in (1, 2, 4):
            @pl.when(jnp.logical_not(takes(way, k)))
            def _():
                slot = (BELOW, ABOVE)[way] + k
                for h in range(HEADS):
                    kv[slot, h, 1 - way] = jnp.zeros((ROWS, DIM), jnp.bfloat16)

    for h in range(HEADS):
        arrived(0, h)
        arrived(1, h)
        for way in (0, 1):
            pass_long(way, 1, h).start()
    for way in (0, 1):
        @pl.when(gives(way, 1))
        def _():
            for h in range(HEADS):
                pass_short(way, 1, h).start()
    for copy in table:
        copy.wait()

    def bias_of(group):
        inside = (group >= 0) & (group < GROUPS)
        row = jnp.clip(group, 0, GROUPS - 1)
        count = jnp.where(inside, counts[0, row], 0)
        first, second = picks[0, row], picks[1, row]
        return [
            jnp.where(((count > 0) & (first == j)) | ((count > 1) & (second == j)), 0.0, -HIDE)
            for j in (0, 1)
        ]

    def attend(h, parts, fresh=False):
        query = qs[h]
        raw, highs = [], []
        for keys, values, biases in parts:
            s = lax.dot_general(
                keys, query, (((1,), (1,)), ((), ())), preferred_element_type=jnp.float32
            )
            for j in (0, 1):
                block = s[j * BLOCK:(j + 1) * BLOCK]
                high = jnp.max(block, axis=0, keepdims=True)
                raw.append(block)
                highs.append(high if biases is None else high + biases[j])
        newest = functools.reduce(jnp.maximum, highs)
        if not fresh:
            newest = jnp.maximum(newest, top[h])
        row_sum, mixed = None, None
        for i, (keys, values, biases) in enumerate(parts):
            weights = []
            for j in (0, 1):
                level = newest if biases is None else newest - biases[j]
                w = jnp.exp2((raw[2 * i + j] - level) * EXPONENT)
                weights.append(w.astype(jnp.bfloat16))
                folded = jnp.sum(w.reshape(BLOCK // 8, 8, ROWS), axis=0)
                row_sum = folded if row_sum is None else row_sum + folded
            weight = jnp.concatenate(weights, axis=0)
            product = lax.dot_general(
                values, weight, (((0,), (0,)), ((), ())), preferred_element_type=jnp.float32
            )
            mixed = product if mixed is None else mixed + product
        if not fresh:
            rescale = jnp.exp2((top[h] - newest) * EXPONENT)
            row_sum = row_sum + total[h] * rescale
            mixed = mixed + acc[h] * rescale
        top[h] = newest
        total[h] = row_sum
        acc[h] = mixed

    def part(slot, h, group):
        return kv[slot, h, 0], kv[slot, h, 1], bias_of(group)

    def over_heads(body):
        def step(h, carry):
            body(h)
            return carry

        lax.fori_loop(0, HEADS, step, 0)

    ZSTEP = NY * NC

    def near(k, h):
        attend(h, [part(BELOW + k, h, me - k * ZSTEP), part(ABOVE + k, h, me + k * ZSTEP)])

    def long_1(h):
        long_hop(1, h)
        pass_on(OWN, SIB, h, sibling).start()
        arrived(2, h)
        attend(h, [(kv[OWN, h, 0], kv[OWN, h, 1], None)], fresh=True)

    def short_1(h):
        short_hop(1, h)
        pass_on(jnp.where(my == NY - 1, BELOW + 1, OWN), M2, h, right).start()
        near(1, h)

    def long_2(h):
        long_hop(2, h)
        pass_on(jnp.where(my == 0, ABOVE + 1, OWN), P2, h, left).start()

    def short_2(h):
        short_hop(2, h)

        @pl.when(my == 2)
        def _():
            pass_on(BELOW + 1, VIA_M4, h, right).start()

        @pl.when(my == 1)
        def _():
            pass_on(ABOVE + 1, VIA_P4, h, left).start()

        near(2, h)

    def long_4(h):
        long_hop(4, h)
        await_slot(M2, h)
        await_slot(P2, h)
        pass_on(jnp.where(core == 1, M2, P2), SIB2, h, sibling).start()

        @pl.when(my == NY - 1)
        def _():
            await_slot(VIA_M4, h)

        pass_on(jnp.where(my == NY - 1, VIA_M4, M2), M4, h, right).start()
        attend(h, [part(M2, h, me - 2), part(P2, h, me + 2)])

    def long_5(h):
        long_hop(5, h)

        @pl.when(my == 0)
        def _():
            await_slot(VIA_P4, h)

        pass_on(jnp.where(my == 0, VIA_P4, P2), P4, h, left).start()

    def long_6(h):
        long_hop(6, h)
        await_slot(SIB, h)
        await_slot(SIB2, h)
        attend(h, [part(SIB, h, me + 1 - 2 * core), part(SIB2, h, me - 1 + 2 * core)])

    def long_7(h):
        long_hop(7, h)
        await_slot(M4, h)
        await_slot(P4, h)
        attend(h, [part(M4, h, me - 4), part(P4, h, me + 4)])

    def short_4(h):
        short_hop(4, h)
        near(4, h)

    over_heads(long_1)
    over_heads(short_1)
    over_heads(long_2)
    over_heads(short_2)
    over_heads(functools.partial(long_hop, 3))
    over_heads(long_4)
    over_heads(long_5)
    over_heads(long_6)
    over_heads(functools.partial(short_hop, 3))
    over_heads(long_7)
    over_heads(short_4)

    def out_columns(x, h):
        return out_hbm.at[:, pl.ds(pl.multiple_of((x * HEADS + h) * DIM, DIM), DIM)]

    def out_rows(x, h):
        return os.at[h, pl.ds(pl.multiple_of(x * TOK, TOK), TOK), :]

    def give_back(h, d):
        target = lax.rem(mx + d, NX)
        return pltpu.make_async_remote_copy(
            src_ref=out_rows(target, h),
            dst_ref=out_columns(mx, h),
            send_sem=out_send.at[h, d - 1],
            recv_sem=out_recv.at[h, d - 1],
            device_id=(me, target),
            device_id_type=MESH,
        )

    def keep_back(h):
        return pltpu.make_async_copy(out_rows(mx, h), out_columns(mx, h), out_local.at[h])

    def eighth(h):
        long_hop(8, h)
        opposite = lax.rem(me + 8 * ZSTEP, GROUPS)
        attend(h, [(far[3, 0, h], far[3, 1, h], bias_of(opposite))])
        row_total = jnp.sum(total[h], axis=0, keepdims=True)
        os[h] = jnp.transpose(acc[h] / row_total).astype(jnp.bfloat16)
        for d in (2, 1, 3):
            give_back(h, d).start()
        keep_back(h).start()

    over_heads(eighth)

    def finish(h):
        for t in (0, 1, 2):
            for d in (1, 2, 3):
                exchange(t, h, d).wait_send()
        for slot in range(M2, VIA_M4):
            pass_on(OWN, slot, h, sibling).wait_send()
        for slot, place in ((VIA_M4, 2), (VIA_P4, 1)):
            @pl.when(my == place)
            def _():
                pass_on(OWN, slot, h, sibling).wait_send()
        for way in (0, 1):
            for k in range(1, 9):
                pass_long(way, k, h).wait_send()
            for k in range(1, 5):
                @pl.when(gives(way, k))
                def _():
                    pass_short(way, k, h).wait_send()
        for d in (1, 2, 3):
            give_back(h, d).wait_send()
        keep_back(h).wait()
        for d in (1, 2, 3):
            there = out_columns(lax.rem(mx + NX - d, NX), h)
            pltpu.make_async_copy(there, there, out_recv.at[h, d - 1]).wait()

    over_heads(finish)


def local(queries, keys, values, block_picks, block_counts):
    picks = jnp.transpose(block_picks, (0, 2, 1))
    dma = pltpu.SemaphoreType.DMA
    return pl.pallas_call(
        kernel,
        out_shape=jax.ShapeDtypeStruct(queries.shape, queries.dtype),
        in_specs=[pl.BlockSpec(memory_space=pltpu.HBM)] * 5,
        out_specs=pl.BlockSpec(memory_space=pl.ANY),
        scratch_shapes=[
            pltpu.VMEM((SLOTS, HEADS, 2, ROWS, DIM), jnp.bfloat16),
            pltpu.VMEM((4, 2, HEADS, ROWS, DIM), jnp.bfloat16),
            pltpu.VMEM((HEADS, ROWS, DIM), jnp.bfloat16),
            pltpu.VMEM((HEADS, ROWS, DIM), jnp.bfloat16),
            pltpu.VMEM((HEADS, DIM, ROWS), jnp.float32),
            pltpu.VMEM((HEADS, 1, ROWS), jnp.float32),
            pltpu.VMEM((HEADS, 8, ROWS), jnp.float32),
            pltpu.SMEM((1, GROUPS), jnp.int32),
            pltpu.SMEM((2, GROUPS), jnp.int32),
            dma((3, HEADS, 3)), dma((3, HEADS, 3)), dma((3, HEADS)),
            dma((SLOTS - M2, HEADS)), dma((SLOTS - M2, HEADS)),
            dma((2, 8, HEADS)), dma((2, 8, HEADS)), dma((2, 4, HEADS)), dma((2, 4, HEADS)),
            dma((HEADS, 3)), dma((HEADS, 3)), dma((HEADS,)), dma((2,)),
        ],
        compiler_params=pltpu.CompilerParams(
            collective_id=0, has_side_effects=True, vmem_limit_bytes=60 * 1024 * 1024
        ),
        name="radial_attention",
    )(queries, keys, values, picks, block_counts)


def solution(mesh):
    placed = P(("frames", "heads"), None)
    return jax.shard_map(
        local,
        mesh=mesh,
        in_specs=(placed, placed, placed, P(), P()),
        out_specs=placed,
        check_vma=False,
    )
```

```python
import functools
import math

import jax
import jax.numpy as jnp
from jax import lax
from jax.experimental import pallas as pl
from jax.experimental.pallas import tpu as pltpu
from jax.sharding import PartitionSpec as P

MESH = pl.DeviceIdType.MESH

NZ, NY, NC, NX = 16, 4, 2, 4
GROUPS = NZ * NY * NC
HEADS = 3
DIM = 128
BLOCK = 128
TOK = 64
ROWS = TOK * NX
HIDE = 1e30
EXPONENT = math.log2(math.e) / math.sqrt(DIM)

OWN = 0
BELOW = 0
ABOVE = 8
M2, P2, M4, P4, SIB, SIB2, VIA_M4, VIA_P4 = 17, 18, 19, 20, 21, 22, 23, 24
SLOTS = 25

STAGES = (
    ("long", 1), ("long", 2), ("long", 3), ("short", 1), ("long", 4), ("long", 5),
    ("short", 2), ("long", 6), ("short", 3), ("long", 7), ("short", 4), ("long", 8),
)


def pick(index, values):
    found = values[-1]
    for i, value in enumerate(values[:-1]):
        found = jnp.where(index == i, value, found)
    return found


def kernel(
    q_hbm, k_hbm, v_hbm, picks_hbm, counts_hbm, out_hbm,
    kv, qs, os, acc, top, total, counts, picks,
    in_send, in_recv, in_local, kv_send, kv_recv, long_send, long_recv, short_send, short_recv,
    out_send, out_recv, out_local, small_sem,
):
    me = lax.axis_index("frames")
    mx = lax.axis_index("heads")
    core = lax.rem(me, NC)
    my = lax.rem(me // NC, NY)
    mz = me // (NC * NY)

    def frame(z, y, c):
        return (z * NY + y) * NC + c

    up = (frame(lax.rem(mz + 1, NZ), my, core), mx)
    down = (frame(lax.rem(mz + NZ - 1, NZ), my, core), mx)
    right = (frame(mz, lax.rem(my + 1, NY), core), mx)
    left = (frame(mz, lax.rem(my + NY - 1, NY), core), mx)
    sibling = (frame(mz, my, 1 - core), mx)
    others = [(me, lax.rem(mx + d, NX)) for d in (1, 2, 3)]

    table = [
        pltpu.make_async_copy(counts_hbm.at[pl.ds(me, 1)], counts, small_sem.at[0]),
        pltpu.make_async_copy(picks_hbm.at[me], picks, small_sem.at[1]),
    ]
    for copy in table:
        copy.start()

    barrier = pltpu.get_barrier_semaphore()
    partners = [up, down, right, left, sibling] + others
    for partner in partners:
        pl.semaphore_signal(barrier, inc=1, device_id=partner, device_id_type=MESH)
    pl.semaphore_wait(barrier, len(partners))

    def landing(t, h, x):
        rows = pl.ds(pl.multiple_of(x * TOK, TOK), TOK)
        if t == 2:
            return qs.at[h, rows, :]
        return kv.at[OWN, h, t, rows, :]

    def piece(t, h, x):
        source = (k_hbm, v_hbm, q_hbm)[t]
        return source.at[:, pl.ds(pl.multiple_of((x * HEADS + h) * DIM, DIM), DIM)]

    def exchange(t, h, d):
        target = lax.rem(mx + d, NX)
        return pltpu.make_async_remote_copy(
            src_ref=piece(t, h, target),
            dst_ref=landing(t, h, mx),
            send_sem=in_send.at[t, h, d - 1],
            recv_sem=in_recv.at[t, h, d - 1],
            device_id=(me, target),
            device_id_type=MESH,
        )

    def kept(t, h):
        return pltpu.make_async_copy(piece(t, h, mx), landing(t, h, mx), in_local.at[t, h])

    def arrived(t, h):
        kept(t, h).wait()
        for d in (1, 2, 3):
            source = lax.rem(mx + NX - d, NX)
            there = landing(t, h, source)
            pltpu.make_async_copy(there, there, in_recv.at[t, h, d - 1]).wait()

    def over_heads(body):
        def step(h, carry):
            body(h)
            return carry

        lax.fori_loop(0, HEADS, step, 0)

    def send_pieces(tensors, h):
        for t in tensors:
            for d in (2, 1, 3):
                exchange(t, h, d).start()
            kept(t, h).start()

    over_heads(functools.partial(send_pieces, (0, 1)))
    over_heads(functools.partial(send_pieces, (2,)))

    def pass_on(source, slot, h, target):
        return pltpu.make_async_remote_copy(
            src_ref=kv.at[source, h],
            dst_ref=kv.at[slot, h],
            send_sem=kv_send.at[slot - M2, h],
            recv_sem=kv_recv.at[slot - M2, h],
            device_id=target,
            device_id_type=MESH,
        )

    def await_slot(slot, h):
        there = kv.at[slot, h]
        pltpu.make_async_copy(there, there, kv_recv.at[slot - M2, h]).wait()

    ways = (up, down)
    depth = (mz, NZ - 1 - mz)

    def held(way, k, h, t):
        return kv.at[jnp.where(k == 0, OWN, (BELOW, ABOVE)[way] + k), h, t]

    def pass_along(way, k, h, t, send, recv):
        return pltpu.make_async_remote_copy(
            src_ref=held(way, k - 1, h, t),
            dst_ref=held(way, k, h, t),
            send_sem=send.at[way, k - 1, h],
            recv_sem=recv.at[way, k - 1, h],
            device_id=ways[way],
            device_id_type=MESH,
        )

    def pass_long(way, k, h):
        return pass_along(way, k, h, way, long_send, long_recv)

    def pass_short(way, k, h):
        return pass_along(way, k, h, 1 - way, short_send, short_recv)

    def takes(way, k):
        d = depth[way]
        return (d >= k) & ((k != 3) | (d <= NZ - 2))

    def gives(way, k):
        d = depth[way]
        return (d >= k - 1) & (d <= jnp.where(k == 3, NZ - 3, NZ - 2))

    def long_hop(k, h):
        for way in (0, 1):
            there = held(way, k, h, way)
            pltpu.make_async_copy(there, there, long_recv.at[way, k - 1, h]).wait()

            @pl.when(k < 8)
            def _():
                pass_long(way, k + 1, h).start()

    def short_hop(k, h):
        for way in (0, 1):
            @pl.when(takes(way, k))
            def _():
                there = held(way, k, h, 1 - way)
                pltpu.make_async_copy(there, there, short_recv.at[way, k - 1, h]).wait()

            @pl.when((k < 4) & gives(way, k + 1))
            def _():
                pass_short(way, k + 1, h).start()

    for way in (0, 1):
        for k in (1, 2, 4):
            @pl.when(jnp.logical_not(takes(way, k)))
            def _():
                slot = (BELOW, ABOVE)[way] + k
                for h in range(HEADS):
                    kv[slot, h, 1 - way] = jnp.zeros((ROWS, DIM), jnp.bfloat16)

    def start_long(h):
        arrived(0, h)
        arrived(1, h)
        for way in (0, 1):
            pass_long(way, 1, h).start()
        pass_on(OWN, SIB, h, sibling).start()

    def start_short(h):
        for way in (0, 1):
            @pl.when(gives(way, 1))
            def _():
                pass_short(way, 1, h).start()

    over_heads(start_long)
    over_heads(start_short)
    for copy in table:
        copy.wait()

    def bias_of(group):
        inside = (group >= 0) & (group < GROUPS)
        row = jnp.clip(group, 0, GROUPS - 1)
        count = jnp.where(inside, counts[0, row], 0)
        first, second = picks[0, row], picks[1, row]
        return [
            jnp.where(
                (group == me) | ((count > 0) & (first == j)) | ((count > 1) & (second == j)), 0.0, -HIDE
            )
            for j in (0, 1)
        ]

    def attend(h, parts):
        query = qs[h]
        raw, biases, highs = [], [], []
        for key_slot, _, group in parts:
            s = lax.dot_general(
                kv[key_slot, h, 0], query, (((1,), (1,)), ((), ())), preferred_element_type=jnp.float32
            )
            for j, bias in enumerate(bias_of(group)):
                block = s[j * BLOCK:(j + 1) * BLOCK]
                raw.append(block)
                biases.append(bias)
                highs.append(jnp.max(block, axis=0, keepdims=True) + bias)
        newest = functools.reduce(jnp.maximum, highs + [top[h]])
        rescale = jnp.exp2((top[h] - newest) * EXPONENT)
        row_sum = total[h] * rescale
        mixed = acc[h] * rescale
        for i, (_, value_slot, _) in enumerate(parts):
            weights = []
            for j in (2 * i, 2 * i + 1):
                w = jnp.exp2((raw[j] - (newest - biases[j])) * EXPONENT)
                weights.append(w.astype(jnp.bfloat16))
                row_sum = row_sum + jnp.sum(w.reshape(BLOCK // 8, 8, ROWS), axis=0)
            mixed = mixed + lax.dot_general(
                kv[value_slot, h, 1], jnp.concatenate(weights, axis=0),
                (((0,), (0,)), ((), ())), preferred_element_type=jnp.float32,
            )
        top[h] = newest
        total[h] = row_sum
        acc[h] = mixed

    top[...] = jnp.full(top.shape, -HIDE, jnp.float32)
    total[...] = jnp.zeros(total.shape, jnp.float32)
    acc[...] = jnp.zeros(acc.shape, jnp.float32)

    zstep = NY * NC
    own_pair = ((OWN, OWN, me), (SIB, SIB, me + 1 - 2 * core))
    far = lax.rem(me + 8 * zstep, GROUPS)
    last_pair = ((SIB2, SIB2, me - 1 + 2 * core), (BELOW + 8, ABOVE + 8, far))

    def near(k):
        return (
            (BELOW + k, BELOW + k, me - k * zstep),
            (ABOVE + k, ABOVE + k, me + k * zstep),
        )

    two_pair = ((M2, M2, me - 2), (P2, P2, me + 2))
    four_pair = ((M4, M4, me - 4), (P4, P4, me + 4))
    pairs = {0: own_pair, 4: near(1), 6: two_pair, 7: near(2), 9: four_pair, 10: near(4), 11: last_pair}

    def chosen(stage, side):
        table = [pairs.get(i, own_pair)[side] for i in range(len(STAGES))]
        return tuple(pick(stage, [entry[field] for entry in table]) for field in range(3))

    def extras(stage, h):
        @pl.when(stage == 0)
        def _():
            arrived(2, h)
            await_slot(SIB, h)

        @pl.when(((stage == 0) & (my < NY - 1)) | ((stage == 3) & (my == NY - 1)))
        def _():
            pass_on(jnp.where(my == NY - 1, BELOW + 1, OWN), M2, h, right).start()

        @pl.when(((stage == 1) & (my > 0)) | ((stage == 3) & (my == 0)))
        def _():
            pass_on(jnp.where(my == 0, ABOVE + 1, OWN), P2, h, left).start()

        @pl.when((stage == 3) & (my == 2))
        def _():
            pass_on(BELOW + 1, VIA_M4, h, right).start()

        @pl.when((stage == 3) & (my == 1))
        def _():
            pass_on(ABOVE + 1, VIA_P4, h, left).start()

        @pl.when(stage == 6)
        def _():
            await_slot(M2, h)
            await_slot(P2, h)
            pass_on(jnp.where(core == 1, M2, P2), SIB2, h, sibling).start()

        @pl.when(stage == 7)
        def _():
            @pl.when(my == NY - 1)
            def _():
                await_slot(VIA_M4, h)

            @pl.when(my == 0)
            def _():
                await_slot(VIA_P4, h)

            pass_on(jnp.where(my == NY - 1, VIA_M4, M2), M4, h, right).start()
            pass_on(jnp.where(my == 0, VIA_P4, P2), P4, h, left).start()

        @pl.when(stage == 9)
        def _():
            await_slot(M4, h)
            await_slot(P4, h)

        @pl.when(stage == 11)
        def _():
            await_slot(SIB2, h)

    def one_stage(stage, carry):
        hop = pick(stage, [k for _, k in STAGES])
        is_long = functools.reduce(
            jnp.logical_and, [stage != i for i, (kind, _) in enumerate(STAGES) if kind == "short"]
        )
        attends = functools.reduce(jnp.logical_or, [stage == i for i in pairs])
        first, second = chosen(stage, 0), chosen(stage, 1)

        def one_head(h):
            @pl.when(is_long)
            def _():
                long_hop(hop, h)

            @pl.when(jnp.logical_not(is_long))
            def _():
                short_hop(hop, h)

            extras(stage, h)

            @pl.when(attends)
            def _():
                attend(h, [first, second])

            @pl.when(stage == len(STAGES) - 1)
            def _():
                finish_head(h)

        over_heads(one_head)
        return carry

    def out_columns(x, h):
        return out_hbm.at[:, pl.ds(pl.multiple_of((x * HEADS + h) * DIM, DIM), DIM)]

    def out_rows(x, h):
        return os.at[h, pl.ds(pl.multiple_of(x * TOK, TOK), TOK), :]

    def give_back(h, d):
        target = lax.rem(mx + d, NX)
        return pltpu.make_async_remote_copy(
            src_ref=out_rows(target, h),
            dst_ref=out_columns(mx, h),
            send_sem=out_send.at[h, d - 1],
            recv_sem=out_recv.at[h, d - 1],
            device_id=(me, target),
            device_id_type=MESH,
        )

    def keep_back(h):
        return pltpu.make_async_copy(out_rows(mx, h), out_columns(mx, h), out_local.at[h])

    def finish_head(h):
        row_total = jnp.sum(total[h], axis=0, keepdims=True)
        os[h] = jnp.transpose(acc[h] / row_total).astype(jnp.bfloat16)
        for d in (2, 1, 3):
            give_back(h, d).start()
        keep_back(h).start()

    lax.fori_loop(0, len(STAGES), one_stage, 0)

    def finish(h):
        for t in (0, 1, 2):
            for d in (1, 2, 3):
                exchange(t, h, d).wait_send()
        for slot in range(M2, VIA_M4):
            pass_on(OWN, slot, h, sibling).wait_send()
        for slot, place in ((VIA_M4, 2), (VIA_P4, 1)):
            @pl.when(my == place)
            def _():
                pass_on(OWN, slot, h, sibling).wait_send()
        for way in (0, 1):
            for k in range(1, 9):
                pass_long(way, k, h).wait_send()
            for k in range(1, 5):
                @pl.when(gives(way, k))
                def _():
                    pass_short(way, k, h).wait_send()
        for d in (1, 2, 3):
            give_back(h, d).wait_send()
        keep_back(h).wait()
        for d in (1, 2, 3):
            there = out_columns(lax.rem(mx + NX - d, NX), h)
            pltpu.make_async_copy(there, there, out_recv.at[h, d - 1]).wait()

    over_heads(finish)


def local(queries, keys, values, block_picks, block_counts):
    picks = jnp.transpose(block_picks, (0, 2, 1))
    dma = pltpu.SemaphoreType.DMA
    return pl.pallas_call(
        kernel,
        out_shape=jax.ShapeDtypeStruct(queries.shape, queries.dtype),
        in_specs=[pl.BlockSpec(memory_space=pltpu.HBM)] * 5,
        out_specs=pl.BlockSpec(memory_space=pl.ANY),
        scratch_shapes=[
            pltpu.VMEM((SLOTS, HEADS, 2, ROWS, DIM), jnp.bfloat16),
            pltpu.VMEM((HEADS, ROWS, DIM), jnp.bfloat16),
            pltpu.VMEM((HEADS, ROWS, DIM), jnp.bfloat16),
            pltpu.VMEM((HEADS, DIM, ROWS), jnp.float32),
            pltpu.VMEM((HEADS, 1, ROWS), jnp.float32),
            pltpu.VMEM((HEADS, 8, ROWS), jnp.float32),
            pltpu.SMEM((1, GROUPS), jnp.int32),
            pltpu.SMEM((2, GROUPS), jnp.int32),
            dma((3, HEADS, 3)), dma((3, HEADS, 3)), dma((3, HEADS)),
            dma((SLOTS - M2, HEADS)), dma((SLOTS - M2, HEADS)),
            dma((2, 8, HEADS)), dma((2, 8, HEADS)), dma((2, 4, HEADS)), dma((2, 4, HEADS)),
            dma((HEADS, 3)), dma((HEADS, 3)), dma((HEADS,)), dma((2,)),
        ],
        compiler_params=pltpu.CompilerParams(
            collective_id=0, has_side_effects=True, vmem_limit_bytes=32 * 1024 * 1024
        ),
        name="radial_attention",
    )(*(pltpu.with_memory_space_constraint(x, pltpu.HBM) for x in (queries, keys, values, picks, block_counts)))


def solution(mesh):
    placed = P(("frames", "heads"), None)
    return jax.shard_map(
        local,
        mesh=mesh,
        in_specs=(placed, placed, placed, P(), P()),
        out_specs=placed,
        check_vma=False,
    )
```

```python
import functools
import math

import jax
import jax.numpy as jnp
from jax import lax
from jax.experimental import pallas as pl
from jax.experimental.pallas import tpu as pltpu
from jax.sharding import PartitionSpec as P

MESH = pl.DeviceIdType.MESH

NZ, NY, NC, NX = 16, 4, 2, 4
GROUPS = NZ * NY * NC
HEADS = 3
DIM = 128
BLOCK = 128
TOK = 64
ROWS = TOK * NX
HIDE = 1e30
EXPONENT = math.log2(math.e) / math.sqrt(DIM)

OWN = 0
BELOW = 0
ABOVE = 8
M2, P2, M4, P4, SIB, SIB2, VIA_M4, VIA_P4 = 17, 18, 19, 20, 21, 22, 23, 24
SLOTS = 25

STAGES = (
    ("long", 1), ("long", 2), ("long", 3), ("short", 1), ("long", 4), ("long", 5),
    ("short", 2), ("long", 6), ("short", 3), ("long", 7), ("short", 4), ("long", 8),
)


def pick(index, values):
    found = values[-1]
    for i, value in enumerate(values[:-1]):
        found = jnp.where(index == i, value, found)
    return found


def kernel(
    q_hbm, k_hbm, v_hbm, picks_hbm, counts_hbm, out_hbm,
    kv, staged, qs, os, acc, top, total, counts, picks,
    in_send, in_recv, in_local, kv_send, kv_recv, long_send, long_recv, short_send, short_recv,
    out_send, out_recv, out_local, small_sem,
):
    me = lax.axis_index("frames")
    mx = lax.axis_index("heads")
    core = lax.rem(me, NC)
    my = lax.rem(me // NC, NY)
    mz = me // (NC * NY)

    def frame(z, y, c):
        return (z * NY + y) * NC + c

    up = (frame(lax.rem(mz + 1, NZ), my, core), mx)
    down = (frame(lax.rem(mz + NZ - 1, NZ), my, core), mx)
    right = (frame(mz, lax.rem(my + 1, NY), core), mx)
    left = (frame(mz, lax.rem(my + NY - 1, NY), core), mx)
    sibling = (frame(mz, my, 1 - core), mx)
    others = [(me, lax.rem(mx + d, NX)) for d in (1, 2, 3)]

    table = [
        pltpu.make_async_copy(counts_hbm.at[pl.ds(me, 1)], counts, small_sem.at[0]),
        pltpu.make_async_copy(picks_hbm.at[me], picks, small_sem.at[1]),
    ]
    staging = [
        pltpu.make_async_copy(source, staged.at[t], small_sem.at[2 + t])
        for t, source in enumerate((k_hbm, v_hbm, q_hbm))
    ]
    for copy in staging + table:
        copy.start()

    barrier = pltpu.get_barrier_semaphore()
    partners = [up, down, right, left, sibling] + others
    for partner in partners:
        pl.semaphore_signal(barrier, inc=1, device_id=partner, device_id_type=MESH)
    pl.semaphore_wait(barrier, len(partners))

    def landing(t, h, x):
        rows = pl.ds(pl.multiple_of(x * TOK, TOK), TOK)
        if t == 2:
            return qs.at[h, rows, :]
        return kv.at[OWN, h, t, rows, :]

    def piece(t, h, x):
        return staged.at[t, :, pl.ds(pl.multiple_of((x * HEADS + h) * DIM, DIM), DIM)]

    def exchange(t, h, d):
        target = lax.rem(mx + d, NX)
        return pltpu.make_async_remote_copy(
            src_ref=piece(t, h, target),
            dst_ref=landing(t, h, mx),
            send_sem=in_send.at[t, h, d - 1],
            recv_sem=in_recv.at[t, h, d - 1],
            device_id=(me, target),
            device_id_type=MESH,
        )

    def kept(t, h):
        return pltpu.make_async_copy(piece(t, h, mx), landing(t, h, mx), in_local.at[t, h])

    def arrived(t, h):
        kept(t, h).wait()
        for d in (1, 2, 3):
            source = lax.rem(mx + NX - d, NX)
            there = landing(t, h, source)
            pltpu.make_async_copy(there, there, in_recv.at[t, h, d - 1]).wait()

    def over_heads(body):
        def step(h, carry):
            body(h)
            return carry

        lax.fori_loop(0, HEADS, step, 0)

    def send_pieces(tensors, h):
        for t in tensors:
            for d in (2, 1, 3):
                exchange(t, h, d).start()
            kept(t, h).start()

    staging[0].wait()
    staging[1].wait()
    send_pieces((0, 1), 0)
    send_pieces((0, 1), 1)

    def pass_on(source, slot, h, target):
        return pltpu.make_async_remote_copy(
            src_ref=kv.at[source, h],
            dst_ref=kv.at[slot, h],
            send_sem=kv_send.at[slot - M2, h],
            recv_sem=kv_recv.at[slot - M2, h],
            device_id=target,
            device_id_type=MESH,
        )

    def await_slot(slot, h):
        there = kv.at[slot, h]
        pltpu.make_async_copy(there, there, kv_recv.at[slot - M2, h]).wait()

    ways = (up, down)
    depth = (mz, NZ - 1 - mz)

    def held(way, k, h, t):
        return kv.at[jnp.where(k == 0, OWN, (BELOW, ABOVE)[way] + k), h, t]

    def pass_along(way, k, h, t, send, recv):
        return pltpu.make_async_remote_copy(
            src_ref=held(way, k - 1, h, t),
            dst_ref=held(way, k, h, t),
            send_sem=send.at[way, k - 1, h],
            recv_sem=recv.at[way, k - 1, h],
            device_id=ways[way],
            device_id_type=MESH,
        )

    def pass_long(way, k, h):
        return pass_along(way, k, h, way, long_send, long_recv)

    def pass_short(way, k, h):
        return pass_along(way, k, h, 1 - way, short_send, short_recv)

    def takes(way, k):
        d = depth[way]
        return (d >= k) & ((k != 3) | (d <= NZ - 2))

    def gives(way, k):
        d = depth[way]
        return (d >= k - 1) & (d <= jnp.where(k == 3, NZ - 3, NZ - 2))

    def long_hop(k, h):
        for way in (0, 1):
            there = held(way, k, h, way)
            pltpu.make_async_copy(there, there, long_recv.at[way, k - 1, h]).wait()

            @pl.when(k < 8)
            def _():
                pass_long(way, k + 1, h).start()

    def short_hop(k, h):
        for way in (0, 1):
            @pl.when(takes(way, k))
            def _():
                there = held(way, k, h, 1 - way)
                pltpu.make_async_copy(there, there, short_recv.at[way, k - 1, h]).wait()

            @pl.when((k < 4) & gives(way, k + 1))
            def _():
                pass_short(way, k + 1, h).start()

    for way in (0, 1):
        for k in (1, 2, 4):
            @pl.when(jnp.logical_not(takes(way, k)))
            def _():
                slot = (BELOW, ABOVE)[way] + k
                for h in range(HEADS):
                    kv[slot, h, 1 - way] = jnp.zeros((ROWS, DIM), jnp.bfloat16)

    def start_long(h):
        for way in (0, 1):
            arrived(way, h)
            pass_long(way, 1, h).start()

    def start_short(h):
        for way in (0, 1):
            @pl.when(gives(way, 1))
            def _():
                pass_short(way, 1, h).start()

    start_long(0)
    send_pieces((0, 1), 2)
    start_long(1)
    start_long(2)
    over_heads(start_short)
    staging[2].wait()
    over_heads(functools.partial(send_pieces, (2,)))
    over_heads(lambda h: pass_on(OWN, SIB, h, sibling).start())
    for copy in table:
        copy.wait()

    def bias_of(group):
        inside = (group >= 0) & (group < GROUPS)
        row = jnp.clip(group, 0, GROUPS - 1)
        count = jnp.where(inside, counts[0, row], 0)
        first, second = picks[0, row], picks[1, row]
        return [
            jnp.where(
                (group == me) | ((count > 0) & (first == j)) | ((count > 1) & (second == j)), 0.0, -HIDE
            )
            for j in (0, 1)
        ]

    def attend(h, parts):
        query = qs[h]
        raw, biases, highs = [], [], []
        for key_slot, _, group in parts:
            s = lax.dot_general(
                kv[key_slot, h, 0], query, (((1,), (1,)), ((), ())), preferred_element_type=jnp.float32
            )
            for j, bias in enumerate(bias_of(group)):
                block = s[j * BLOCK:(j + 1) * BLOCK]
                raw.append(block)
                biases.append(bias)
                highs.append(jnp.max(block, axis=0, keepdims=True) + bias)
        newest = functools.reduce(jnp.maximum, highs + [top[h]])
        rescale = jnp.exp2((top[h] - newest) * EXPONENT)
        row_sum = total[h] * rescale
        mixed = acc[h] * rescale
        for i, (_, value_slot, _) in enumerate(parts):
            weights = []
            for j in (2 * i, 2 * i + 1):
                w = jnp.exp2((raw[j] - (newest - biases[j])) * EXPONENT)
                weights.append(w.astype(jnp.bfloat16))
                row_sum = row_sum + jnp.sum(w.reshape(BLOCK // 8, 8, ROWS), axis=0)
            mixed = mixed + lax.dot_general(
                kv[value_slot, h, 1], jnp.concatenate(weights, axis=0),
                (((0,), (0,)), ((), ())), preferred_element_type=jnp.float32,
            )
        top[h] = newest
        total[h] = row_sum
        acc[h] = mixed

    top[...] = jnp.full(top.shape, -HIDE, jnp.float32)
    total[...] = jnp.zeros(total.shape, jnp.float32)
    acc[...] = jnp.zeros(acc.shape, jnp.float32)

    zstep = NY * NC
    own_pair = ((OWN, OWN, me), (SIB, SIB, me + 1 - 2 * core))
    far = lax.rem(me + 8 * zstep, GROUPS)
    last_pair = ((SIB2, SIB2, me - 1 + 2 * core), (BELOW + 8, ABOVE + 8, far))

    def near(k):
        return (
            (BELOW + k, BELOW + k, me - k * zstep),
            (ABOVE + k, ABOVE + k, me + k * zstep),
        )

    two_pair = ((M2, M2, me - 2), (P2, P2, me + 2))
    four_pair = ((M4, M4, me - 4), (P4, P4, me + 4))
    pairs = {0: own_pair, 4: near(1), 6: two_pair, 7: near(2), 9: four_pair, 10: near(4), 11: last_pair}

    def chosen(stage, side):
        table = [pairs.get(i, own_pair)[side] for i in range(len(STAGES))]
        return tuple(pick(stage, [entry[field] for entry in table]) for field in range(3))

    def extras(stage, h):
        @pl.when(stage == 0)
        def _():
            arrived(2, h)
            await_slot(SIB, h)

        @pl.when(((stage == 0) & (my < NY - 1)) | ((stage == 3) & (my == NY - 1)))
        def _():
            pass_on(jnp.where(my == NY - 1, BELOW + 1, OWN), M2, h, right).start()

        @pl.when(((stage == 1) & (my > 0)) | ((stage == 3) & (my == 0)))
        def _():
            pass_on(jnp.where(my == 0, ABOVE + 1, OWN), P2, h, left).start()

        @pl.when((stage == 3) & (my == 2))
        def _():
            pass_on(BELOW + 1, VIA_M4, h, right).start()

        @pl.when((stage == 3) & (my == 1))
        def _():
            pass_on(ABOVE + 1, VIA_P4, h, left).start()

        @pl.when(stage == 6)
        def _():
            await_slot(M2, h)
            await_slot(P2, h)
            pass_on(jnp.where(core == 1, M2, P2), SIB2, h, sibling).start()

        @pl.when(stage == 7)
        def _():
            @pl.when(my == NY - 1)
            def _():
                await_slot(VIA_M4, h)

            @pl.when(my == 0)
            def _():
                await_slot(VIA_P4, h)

            pass_on(jnp.where(my == NY - 1, VIA_M4, M2), M4, h, right).start()
            pass_on(jnp.where(my == 0, VIA_P4, P2), P4, h, left).start()

        @pl.when(stage == 8)
        def _():
            for t in (0, 1, 2):
                for d in (1, 2, 3):
                    exchange(t, h, d).wait_send()
            release(h, (SIB, M2, P2), (1, 2, 3, 4, 5), (1, 2))
            for slot, place in ((VIA_M4, 2), (VIA_P4, 1)):
                @pl.when(my == place)
                def _():
                    pass_on(OWN, slot, h, sibling).wait_send()

        @pl.when(stage == 9)
        def _():
            await_slot(M4, h)
            await_slot(P4, h)

        @pl.when(stage == 11)
        def _():
            await_slot(SIB2, h)

    def release(h, slots, long_hops, short_hops):
        for slot in slots:
            pass_on(OWN, slot, h, sibling).wait_send()
        for way in (0, 1):
            for k in long_hops:
                pass_long(way, k, h).wait_send()
            for k in short_hops:
                @pl.when(gives(way, k))
                def _():
                    pass_short(way, k, h).wait_send()

    def one_stage(stage, carry):
        hop = pick(stage, [k for _, k in STAGES])
        is_long = functools.reduce(
            jnp.logical_and, [stage != i for i, (kind, _) in enumerate(STAGES) if kind == "short"]
        )
        attends = functools.reduce(jnp.logical_or, [stage == i for i in pairs])
        first, second = chosen(stage, 0), chosen(stage, 1)

        def one_head(h):
            @pl.when(is_long)
            def _():
                long_hop(hop, h)

            @pl.when(jnp.logical_not(is_long))
            def _():
                short_hop(hop, h)

            extras(stage, h)

            @pl.when(attends)
            def _():
                attend(h, [first, second])

            @pl.when(stage == len(STAGES) - 1)
            def _():
                finish_head(h)

        over_heads(one_head)
        return carry

    def out_columns(x, h):
        return out_hbm.at[:, pl.ds(pl.multiple_of((x * HEADS + h) * DIM, DIM), DIM)]

    def out_rows(x, h):
        return os.at[h, pl.ds(pl.multiple_of(x * TOK, TOK), TOK), :]

    def give_back(h, d):
        target = lax.rem(mx + d, NX)
        return pltpu.make_async_remote_copy(
            src_ref=out_rows(target, h),
            dst_ref=out_columns(mx, h),
            send_sem=out_send.at[h, d - 1],
            recv_sem=out_recv.at[h, d - 1],
            device_id=(me, target),
            device_id_type=MESH,
        )

    def keep_back(h):
        return pltpu.make_async_copy(out_rows(mx, h), out_columns(mx, h), out_local.at[h])

    def finish_head(h):
        row_total = jnp.sum(total[h], axis=0, keepdims=True)
        os[h] = jnp.transpose(acc[h] / row_total).astype(jnp.bfloat16)
        for d in (2, 1, 3):
            give_back(h, d).start()
        keep_back(h).start()

    lax.fori_loop(0, len(STAGES), one_stage, 0)

    def finish(h):
        release(h, (M4, P4, SIB2), (6, 7, 8), (3, 4))
        for d in (1, 2, 3):
            give_back(h, d).wait_send()
        keep_back(h).wait()
        for d in (1, 2, 3):
            there = out_columns(lax.rem(mx + NX - d, NX), h)
            pltpu.make_async_copy(there, there, out_recv.at[h, d - 1]).wait()

    over_heads(finish)


def local(queries, keys, values, block_picks, block_counts):
    picks = jnp.transpose(block_picks, (0, 2, 1))
    dma = pltpu.SemaphoreType.DMA
    return pl.pallas_call(
        kernel,
        out_shape=jax.ShapeDtypeStruct(queries.shape, queries.dtype),
        in_specs=[pl.BlockSpec(memory_space=pltpu.HBM)] * 5,
        out_specs=pl.BlockSpec(memory_space=pl.ANY),
        scratch_shapes=[
            pltpu.VMEM((SLOTS, HEADS, 2, ROWS, DIM), jnp.bfloat16),
            pltpu.VMEM((3,) + queries.shape, jnp.bfloat16),
            pltpu.VMEM((HEADS, ROWS, DIM), jnp.bfloat16),
            pltpu.VMEM((HEADS, ROWS, DIM), jnp.bfloat16),
            pltpu.VMEM((HEADS, DIM, ROWS), jnp.float32),
            pltpu.VMEM((HEADS, 1, ROWS), jnp.float32),
            pltpu.VMEM((HEADS, 8, ROWS), jnp.float32),
            pltpu.SMEM((1, GROUPS), jnp.int32),
            pltpu.SMEM((2, GROUPS), jnp.int32),
            dma((3, HEADS, 3)), dma((3, HEADS, 3)), dma((3, HEADS)),
            dma((SLOTS - M2, HEADS)), dma((SLOTS - M2, HEADS)),
            dma((2, 8, HEADS)), dma((2, 8, HEADS)), dma((2, 4, HEADS)), dma((2, 4, HEADS)),
            dma((HEADS, 3)), dma((HEADS, 3)), dma((HEADS,)), dma((5,)),
        ],
        compiler_params=pltpu.CompilerParams(
            collective_id=0, has_side_effects=True, vmem_limit_bytes=32 * 1024 * 1024
        ),
        name="radial_attention",
    )(*(pltpu.with_memory_space_constraint(x, pltpu.HBM) for x in (queries, keys, values, picks, block_counts)))


def solution(mesh):
    placed = P(("frames", "heads"), None)
    return jax.shard_map(
        local,
        mesh=mesh,
        in_specs=(placed, placed, placed, P(), P()),
        out_specs=placed,
        check_vma=False,
    )
```

```python
import functools
import math

import jax
import jax.numpy as jnp
from jax import lax
from jax.experimental import pallas as pl
from jax.experimental.pallas import tpu as pltpu
from jax.sharding import PartitionSpec as P

MESH = pl.DeviceIdType.MESH

NZ, NY, NC, NX = 16, 4, 2, 4
GROUPS = NZ * NY * NC
HEADS = 3
DIM = 128
BLOCK = 128
TOK = 64
ROWS = TOK * NX
HIDE = 1e30
EXPONENT = math.log2(math.e) / math.sqrt(DIM)

OWN = 0
BELOW = 0
ABOVE = 8
M2, P2, M4, P4, SIB, SIB2, VIA_M4, VIA_P4 = 17, 18, 19, 20, 21, 22, 23, 24
SLOTS = 25

STAGES = (
    ("long", 1), ("long", 2), ("long", 3), ("short", 1), ("long", 4), ("long", 5),
    ("short", 2), ("long", 6), ("short", 3), ("long", 7), ("short", 4), ("long", 8),
)


def pick(index, values):
    found = values[-1]
    for i, value in enumerate(values[:-1]):
        found = jnp.where(index == i, value, found)
    return found


def kernel(
    q_hbm, k_hbm, v_hbm, picks_hbm, counts_hbm, out_hbm,
    kv, staged, qs, os, acc, top, total, counts, picks,
    in_send, in_recv, in_local, kv_send, kv_recv, long_send, long_recv, short_send, short_recv,
    out_send, out_recv, out_local, small_sem,
):
    me = lax.axis_index("frames")
    mx = lax.axis_index("heads")
    core = lax.rem(me, NC)
    my = lax.rem(me // NC, NY)
    mz = me // (NC * NY)

    def frame(z, y, c):
        return (z * NY + y) * NC + c

    up = (frame(lax.rem(mz + 1, NZ), my, core), mx)
    down = (frame(lax.rem(mz + NZ - 1, NZ), my, core), mx)
    right = (frame(mz, lax.rem(my + 1, NY), core), mx)
    left = (frame(mz, lax.rem(my + NY - 1, NY), core), mx)
    sibling = (frame(mz, my, 1 - core), mx)
    others = [(me, lax.rem(mx + d, NX)) for d in (1, 2, 3)]

    table = [
        pltpu.make_async_copy(counts_hbm.at[pl.ds(me, 1)], counts, small_sem.at[0]),
        pltpu.make_async_copy(picks_hbm.at[me], picks, small_sem.at[1]),
    ]
    staging = [
        pltpu.make_async_copy(source, staged.at[t], small_sem.at[2 + t])
        for t, source in enumerate((k_hbm, v_hbm, q_hbm))
    ]
    for copy in staging + table:
        copy.start()

    barrier = pltpu.get_barrier_semaphore()
    partners = [up, down, right, left, sibling] + others
    for partner in partners:
        pl.semaphore_signal(barrier, inc=1, device_id=partner, device_id_type=MESH)
    pl.semaphore_wait(barrier, len(partners))

    def landing(t, h, x):
        rows = pl.ds(pl.multiple_of(x * TOK, TOK), TOK)
        if t == 2:
            return qs.at[h, rows, :]
        return kv.at[OWN, h, t, rows, :]

    def piece(t, h, x):
        return staged.at[t, :, pl.ds(pl.multiple_of((x * HEADS + h) * DIM, DIM), DIM)]

    def exchange(t, h, d):
        target = lax.rem(mx + d, NX)
        return pltpu.make_async_remote_copy(
            src_ref=piece(t, h, target),
            dst_ref=landing(t, h, mx),
            send_sem=in_send.at[t, h, d - 1],
            recv_sem=in_recv.at[t, h, d - 1],
            device_id=(me, target),
            device_id_type=MESH,
        )

    def kept(t, h):
        return pltpu.make_async_copy(piece(t, h, mx), landing(t, h, mx), in_local.at[t, h])

    def arrived(t, h):
        kept(t, h).wait()
        for d in (1, 2, 3):
            source = lax.rem(mx + NX - d, NX)
            there = landing(t, h, source)
            pltpu.make_async_copy(there, there, in_recv.at[t, h, d - 1]).wait()

    def over_heads(body):
        def step(h, carry):
            body(h)
            return carry

        lax.fori_loop(0, HEADS, step, 0)

    def send_pieces(tensors, h):
        for t in tensors:
            for d in (2, 1, 3):
                exchange(t, h, d).start()
            kept(t, h).start()

    def pass_on(source, slot, h, target):
        return pltpu.make_async_remote_copy(
            src_ref=kv.at[source, h],
            dst_ref=kv.at[slot, h],
            send_sem=kv_send.at[slot - M2, h],
            recv_sem=kv_recv.at[slot - M2, h],
            device_id=target,
            device_id_type=MESH,
        )

    def await_slot(slot, h):
        there = kv.at[slot, h]
        pltpu.make_async_copy(there, there, kv_recv.at[slot - M2, h]).wait()

    ways = (up, down)
    depth = (mz, NZ - 1 - mz)

    def held(way, k, h, t):
        return kv.at[jnp.where(k == 0, OWN, (BELOW, ABOVE)[way] + k), h, t]

    def pass_along(way, k, h, t, send, recv):
        return pltpu.make_async_remote_copy(
            src_ref=held(way, k - 1, h, t),
            dst_ref=held(way, k, h, t),
            send_sem=send.at[way, k - 1, h],
            recv_sem=recv.at[way, k - 1, h],
            device_id=ways[way],
            device_id_type=MESH,
        )

    def pass_long(way, k, h):
        return pass_along(way, k, h, way, long_send, long_recv)

    def pass_short(way, k, h):
        return pass_along(way, k, h, 1 - way, short_send, short_recv)

    def takes(way, k):
        d = depth[way]
        return (d >= k) & ((k != 3) | (d <= NZ - 2))

    def gives(way, k):
        d = depth[way]
        return (d >= k - 1) & (d <= jnp.where(k == 3, NZ - 3, NZ - 2))

    def long_hop(k, h):
        for way in (0, 1):
            there = held(way, k, h, way)
            pltpu.make_async_copy(there, there, long_recv.at[way, k - 1, h]).wait()

            @pl.when(k < 8)
            def _():
                pass_long(way, k + 1, h).start()

    def short_hop(k, h):
        for way in (0, 1):
            @pl.when(takes(way, k))
            def _():
                there = held(way, k, h, 1 - way)
                pltpu.make_async_copy(there, there, short_recv.at[way, k - 1, h]).wait()

            @pl.when((k < 4) & gives(way, k + 1))
            def _():
                pass_short(way, k + 1, h).start()

    for way in (0, 1):
        for k in (1, 2, 4):
            @pl.when(jnp.logical_not(takes(way, k)))
            def _():
                slot = (BELOW, ABOVE)[way] + k
                for h in range(HEADS):
                    kv[slot, h, 1 - way] = jnp.zeros((ROWS, DIM), jnp.bfloat16)

    def first_hop(way, h, t, x, source):
        rows = pl.ds(pl.multiple_of(x * TOK, TOK), TOK)
        send, recv = (long_send, long_recv) if t == way else (short_send, short_recv)
        return pltpu.make_async_remote_copy(
            src_ref=source,
            dst_ref=held(way, 1, h, t).at[rows],
            send_sem=send.at[way, 0, h],
            recv_sem=recv.at[way, 0, h],
            device_id=ways[way],
            device_id_type=MESH,
        )

    def own_long(h):
        for way in (0, 1):
            first_hop(way, h, way, mx, piece(way, h, mx)).start()

    def own_short(h):
        for way in (0, 1):
            @pl.when(gives(way, 1))
            def _():
                first_hop(way, h, 1 - way, mx, piece(1 - way, h, mx)).start()

    def start_long(h):
        for d in (1, 3, 2):
            x = lax.rem(mx + NX - d, NX)
            for way in (0, 1):
                there = landing(way, h, x)
                pltpu.make_async_copy(there, there, in_recv.at[way, h, d - 1]).wait()
                first_hop(way, h, way, x, there).start()

    def start_short(h):
        for d in (1, 3, 2):
            x = lax.rem(mx + NX - d, NX)
            for way in (0, 1):
                @pl.when(gives(way, 1))
                def _():
                    first_hop(way, h, 1 - way, x, landing(1 - way, h, x)).start()

    staging[0].wait()
    staging[1].wait()
    send_pieces((0, 1), 0)
    over_heads(own_long)
    send_pieces((0, 1), 1)
    send_pieces((0, 1), 2)
    over_heads(own_short)
    over_heads(start_long)
    over_heads(start_short)
    staging[2].wait()
    over_heads(functools.partial(send_pieces, (2,)))

    def start_sibling(h):
        kept(0, h).wait()
        kept(1, h).wait()
        pass_on(OWN, SIB, h, sibling).start()

    over_heads(start_sibling)
    for copy in table:
        copy.wait()

    def bias_of(group):
        inside = (group >= 0) & (group < GROUPS)
        row = jnp.clip(group, 0, GROUPS - 1)
        count = jnp.where(inside, counts[0, row], 0)
        first, second = picks[0, row], picks[1, row]
        return [
            jnp.where(
                (group == me) | ((count > 0) & (first == j)) | ((count > 1) & (second == j)), 0.0, -HIDE
            )
            for j in (0, 1)
        ]

    def attend(h, parts):
        query = qs[h]
        raw, biases, highs = [], [], []
        for key_slot, _, group in parts:
            s = lax.dot_general(
                kv[key_slot, h, 0], query, (((1,), (1,)), ((), ())), preferred_element_type=jnp.float32
            )
            for j, bias in enumerate(bias_of(group)):
                block = s[j * BLOCK:(j + 1) * BLOCK]
                raw.append(block)
                biases.append(bias)
                highs.append(jnp.max(block, axis=0, keepdims=True) + bias)
        newest = functools.reduce(jnp.maximum, highs + [top[h]])
        rescale = jnp.exp2((top[h] - newest) * EXPONENT)
        row_sum = total[h] * rescale
        mixed = acc[h] * rescale
        for i, (_, value_slot, _) in enumerate(parts):
            weights = []
            for j in (2 * i, 2 * i + 1):
                w = jnp.exp2((raw[j] - (newest - biases[j])) * EXPONENT)
                weights.append(w.astype(jnp.bfloat16))
                row_sum = row_sum + jnp.sum(w.reshape(BLOCK // 8, 8, ROWS), axis=0)
            mixed = mixed + lax.dot_general(
                kv[value_slot, h, 1], jnp.concatenate(weights, axis=0),
                (((0,), (0,)), ((), ())), preferred_element_type=jnp.float32,
            )
        top[h] = newest
        total[h] = row_sum
        acc[h] = mixed

    top[...] = jnp.full(top.shape, -HIDE, jnp.float32)
    total[...] = jnp.zeros(total.shape, jnp.float32)
    acc[...] = jnp.zeros(acc.shape, jnp.float32)

    zstep = NY * NC
    own_pair = ((OWN, OWN, me), (SIB, SIB, me + 1 - 2 * core))
    far = lax.rem(me + 8 * zstep, GROUPS)
    sib2 = (SIB2, SIB2, me - 1 + 2 * core)
    opposite = (BELOW + 8, ABOVE + 8, far)

    def near(k):
        return (
            (BELOW + k, BELOW + k, me - k * zstep),
            (ABOVE + k, ABOVE + k, me + k * zstep),
        )

    two_pair = ((M2, M2, me - 2), (P2, P2, me + 2))
    four_pair = ((M4, M4, me - 4), (P4, P4, me + 4))
    pairs = {0: own_pair, 4: near(1), 6: two_pair, 7: near(2), 9: four_pair, 10: near(4)}
    singles = {8: sib2, 11: opposite}

    def chosen(stage, side):
        table = [pairs.get(i, own_pair)[side] for i in range(len(STAGES))]
        return tuple(pick(stage, [entry[field] for entry in table]) for field in range(3))

    def extras(stage, h):
        @pl.when(stage == 0)
        def _():
            arrived(2, h)
            await_slot(SIB, h)

        @pl.when(((stage == 0) & (my < NY - 1)) | ((stage == 3) & (my == NY - 1)))
        def _():
            pass_on(jnp.where(my == NY - 1, BELOW + 1, OWN), M2, h, right).start()

        @pl.when(((stage == 1) & (my > 0)) | ((stage == 3) & (my == 0)))
        def _():
            pass_on(jnp.where(my == 0, ABOVE + 1, OWN), P2, h, left).start()

        @pl.when((stage == 3) & (my == 2))
        def _():
            pass_on(BELOW + 1, VIA_M4, h, right).start()

        @pl.when((stage == 3) & (my == 1))
        def _():
            pass_on(ABOVE + 1, VIA_P4, h, left).start()

        @pl.when(stage == 6)
        def _():
            await_slot(M2, h)
            await_slot(P2, h)
            pass_on(jnp.where(core == 1, M2, P2), SIB2, h, sibling).start()

        @pl.when(stage == 7)
        def _():
            @pl.when(my == NY - 1)
            def _():
                await_slot(VIA_M4, h)

            @pl.when(my == 0)
            def _():
                await_slot(VIA_P4, h)

            pass_on(jnp.where(my == NY - 1, VIA_M4, M2), M4, h, right).start()
            pass_on(jnp.where(my == 0, VIA_P4, P2), P4, h, left).start()

        @pl.when(stage == 8)
        def _():
            await_slot(SIB2, h)
            for t in (0, 1, 2):
                for d in (1, 2, 3):
                    exchange(t, h, d).wait_send()
            release(h, (SIB, M2, P2), (1, 2, 3, 4, 5), (1, 2))
            for slot, place in ((VIA_M4, 2), (VIA_P4, 1)):
                @pl.when(my == place)
                def _():
                    pass_on(OWN, slot, h, sibling).wait_send()

        @pl.when(stage == 9)
        def _():
            await_slot(M4, h)
            await_slot(P4, h)


    def release(h, slots, long_hops, short_hops):
        for slot in slots:
            pass_on(OWN, slot, h, sibling).wait_send()
        for way in (0, 1):
            for k in long_hops:
                pass_long(way, k, h).wait_send()
            for k in short_hops:
                @pl.when(gives(way, k))
                def _():
                    pass_short(way, k, h).wait_send()

    def one_stage(stage, carry):
        hop = pick(stage, [k for _, k in STAGES])
        is_long = functools.reduce(
            jnp.logical_and, [stage != i for i, (kind, _) in enumerate(STAGES) if kind == "short"]
        )
        attends = functools.reduce(jnp.logical_or, [stage == i for i in pairs])
        first, second = chosen(stage, 0), chosen(stage, 1)
        alone = functools.reduce(jnp.logical_or, [stage == i for i in singles])
        single = tuple(jnp.where(stage == 8, *entry) for entry in zip(sib2, opposite))

        def one_head(h):
            @pl.when(is_long)
            def _():
                long_hop(hop, h)

            @pl.when(jnp.logical_not(is_long))
            def _():
                short_hop(hop, h)

            extras(stage, h)

            @pl.when(attends)
            def _():
                attend(h, [first, second])

            @pl.when(alone)
            def _():
                attend(h, [single])

            @pl.when(stage == len(STAGES) - 1)
            def _():
                finish_head(h)

        over_heads(one_head)
        return carry

    def out_columns(x, h):
        return out_hbm.at[:, pl.ds(pl.multiple_of((x * HEADS + h) * DIM, DIM), DIM)]

    def out_rows(x, h):
        return os.at[h, pl.ds(pl.multiple_of(x * TOK, TOK), TOK), :]

    def give_back(h, d):
        target = lax.rem(mx + d, NX)
        return pltpu.make_async_remote_copy(
            src_ref=out_rows(target, h),
            dst_ref=out_columns(mx, h),
            send_sem=out_send.at[h, d - 1],
            recv_sem=out_recv.at[h, d - 1],
            device_id=(me, target),
            device_id_type=MESH,
        )

    def keep_back(h):
        return pltpu.make_async_copy(out_rows(mx, h), out_columns(mx, h), out_local.at[h])

    def finish_head(h):
        row_total = jnp.sum(total[h], axis=0, keepdims=True)
        os[h] = jnp.transpose(acc[h] / row_total).astype(jnp.bfloat16)
        for d in (2, 1, 3):
            give_back(h, d).start()
        keep_back(h).start()

    lax.fori_loop(0, len(STAGES), one_stage, 0)

    def finish(h):
        release(h, (M4, P4, SIB2), (6, 7, 8), (3, 4))
        for d in (1, 2, 3):
            give_back(h, d).wait_send()
        keep_back(h).wait()
        for d in (1, 2, 3):
            there = out_columns(lax.rem(mx + NX - d, NX), h)
            pltpu.make_async_copy(there, there, out_recv.at[h, d - 1]).wait()

    over_heads(finish)


def local(queries, keys, values, block_picks, block_counts):
    picks = jnp.transpose(block_picks, (0, 2, 1))
    dma = pltpu.SemaphoreType.DMA
    return pl.pallas_call(
        kernel,
        out_shape=jax.ShapeDtypeStruct(queries.shape, queries.dtype),
        in_specs=[pl.BlockSpec(memory_space=pltpu.HBM)] * 5,
        out_specs=pl.BlockSpec(memory_space=pl.ANY),
        scratch_shapes=[
            pltpu.VMEM((SLOTS, HEADS, 2, ROWS, DIM), jnp.bfloat16),
            pltpu.VMEM((3,) + queries.shape, jnp.bfloat16),
            pltpu.VMEM((HEADS, ROWS, DIM), jnp.bfloat16),
            pltpu.VMEM((HEADS, ROWS, DIM), jnp.bfloat16),
            pltpu.VMEM((HEADS, DIM, ROWS), jnp.float32),
            pltpu.VMEM((HEADS, 1, ROWS), jnp.float32),
            pltpu.VMEM((HEADS, 8, ROWS), jnp.float32),
            pltpu.SMEM((1, GROUPS), jnp.int32),
            pltpu.SMEM((2, GROUPS), jnp.int32),
            dma((3, HEADS, 3)), dma((3, HEADS, 3)), dma((3, HEADS)),
            dma((SLOTS - M2, HEADS)), dma((SLOTS - M2, HEADS)),
            dma((2, 8, HEADS)), dma((2, 8, HEADS)), dma((2, 4, HEADS)), dma((2, 4, HEADS)),
            dma((HEADS, 3)), dma((HEADS, 3)), dma((HEADS,)), dma((5,)),
        ],
        compiler_params=pltpu.CompilerParams(
            collective_id=0, has_side_effects=True, vmem_limit_bytes=32 * 1024 * 1024
        ),
        name="radial_attention",
    )(*(pltpu.with_memory_space_constraint(x, pltpu.HBM) for x in (queries, keys, values, picks, block_counts)))


def solution(mesh):
    placed = P(("frames", "heads"), None)
    return jax.shard_map(
        local,
        mesh=mesh,
        in_specs=(placed, placed, placed, P(), P()),
        out_specs=placed,
        check_vma=False,
    )
```

```python
import functools
import math

import jax
import jax.numpy as jnp
from jax import lax
from jax.experimental import pallas as pl
from jax.experimental.pallas import tpu as pltpu
from jax.sharding import PartitionSpec as P

MESH = pl.DeviceIdType.MESH

NZ, NY, NC, NX = 16, 4, 2, 4
GROUPS = NZ * NY * NC
HEADS = 3
DIM = 128
BLOCK = 128
TOK = 64
ROWS = TOK * NX
HIDE = 1e30
EXPONENT = math.log2(math.e) / math.sqrt(DIM)

OWN = 0
BELOW = 0
ABOVE = 8
M2, P2, M4, P4, SIB, SIB2, VIA_M4, VIA_P4 = 17, 18, 19, 20, 21, 22, 23, 24
SLOTS = 25

STAGES = 12
ORDER = (
    (
        (3, 4, 5, 7), (3, 3, 4, 5), (2, 4, 4, 6), (2, 4, 5, 7),
        (3, 5, 6, 7), (3, 4, 6, 7), (3, 5, 6, 7), (2, 5, 6, 7),
        (2, 5, 5, 7), (3, 5, 6, 7), (3, 5, 6, 7), (3, 5, 6, 7),
        (3, 5, 6, 7), (3, 5, 6, 7), (3, 5, 6, 7), (3, 5, 6, 7),
    ),
    (
        (3, 4, 7, 7), (3, 5, 6, 7), (2, 5, 6, 7), (1, 4, 6, 7),
        (3, 5, 6, 7), (2, 4, 6, 7), (3, 5, 6, 7), (2, 4, 5, 7),
        (1, 4, 6, 7), (3, 5, 6, 7), (3, 5, 6, 7), (3, 5, 6, 7),
        (3, 5, 6, 7), (3, 5, 6, 7), (3, 5, 6, 7), (3, 5, 6, 7),
    ),
)


def pick(index, values):
    found = values[-1]
    for i, value in enumerate(values[:-1]):
        found = jnp.where(index == i, value, found)
    return found


def kernel(
    q_hbm, k_hbm, v_hbm, picks_hbm, counts_hbm, out_hbm,
    kv, staged, qs, os, acc, top, total, counts, picks,
    in_send, in_recv, in_local, kv_send, kv_recv, long_send, long_recv, short_send, short_recv,
    out_send, out_recv, out_local, small_sem,
):
    me = lax.axis_index("frames")
    mx = lax.axis_index("heads")
    core = lax.rem(me, NC)
    my = lax.rem(me // NC, NY)
    mz = me // (NC * NY)

    def frame(z, y, c):
        return (z * NY + y) * NC + c

    up = (frame(lax.rem(mz + 1, NZ), my, core), mx)
    down = (frame(lax.rem(mz + NZ - 1, NZ), my, core), mx)
    right = (frame(mz, lax.rem(my + 1, NY), core), mx)
    left = (frame(mz, lax.rem(my + NY - 1, NY), core), mx)
    sibling = (frame(mz, my, 1 - core), mx)
    others = [(me, lax.rem(mx + d, NX)) for d in (1, 2, 3)]

    table = [
        pltpu.make_async_copy(counts_hbm.at[pl.ds(me, 1)], counts, small_sem.at[0]),
        pltpu.make_async_copy(picks_hbm.at[me], picks, small_sem.at[1]),
    ]
    staging = [
        pltpu.make_async_copy(source, staged.at[t], small_sem.at[2 + t])
        for t, source in enumerate((k_hbm, v_hbm, q_hbm))
    ]
    for copy in staging + table:
        copy.start()

    barrier = pltpu.get_barrier_semaphore()
    partners = [up, down, right, left, sibling] + others
    for partner in partners:
        pl.semaphore_signal(barrier, inc=1, device_id=partner, device_id_type=MESH)
    pl.semaphore_wait(barrier, len(partners))

    def landing(t, h, x):
        rows = pl.ds(pl.multiple_of(x * TOK, TOK), TOK)
        if t == 2:
            return qs.at[h, rows, :]
        return kv.at[OWN, h, t, rows, :]

    def piece(t, h, x):
        return staged.at[t, :, pl.ds(pl.multiple_of((x * HEADS + h) * DIM, DIM), DIM)]

    def exchange(t, h, d):
        target = lax.rem(mx + d, NX)
        return pltpu.make_async_remote_copy(
            src_ref=piece(t, h, target),
            dst_ref=landing(t, h, mx),
            send_sem=in_send.at[t, h, d - 1],
            recv_sem=in_recv.at[t, h, d - 1],
            device_id=(me, target),
            device_id_type=MESH,
        )

    def kept(t, h):
        return pltpu.make_async_copy(piece(t, h, mx), landing(t, h, mx), in_local.at[t, h])

    def arrived(t, h):
        kept(t, h).wait()
        for d in (1, 2, 3):
            source = lax.rem(mx + NX - d, NX)
            there = landing(t, h, source)
            pltpu.make_async_copy(there, there, in_recv.at[t, h, d - 1]).wait()

    def over_heads(body):
        def step(h, carry):
            body(h)
            return carry

        lax.fori_loop(0, HEADS, step, 0)

    def send_pieces(tensors, h):
        for t in tensors:
            for d in (2, 1, 3):
                exchange(t, h, d).start()
            kept(t, h).start()

    def pass_on(source, slot, h, target):
        return pltpu.make_async_remote_copy(
            src_ref=kv.at[source, h],
            dst_ref=kv.at[slot, h],
            send_sem=kv_send.at[slot - M2, h],
            recv_sem=kv_recv.at[slot - M2, h],
            device_id=target,
            device_id_type=MESH,
        )

    def await_slot(slot, h):
        there = kv.at[slot, h]
        pltpu.make_async_copy(there, there, kv_recv.at[slot - M2, h]).wait()

    ways = (up, down)
    depth = (mz, NZ - 1 - mz)

    def held(way, k, h, t):
        return kv.at[jnp.where(k == 0, OWN, (BELOW, ABOVE)[way] + k), h, t]

    def pass_along(way, k, h, t, send, recv):
        return pltpu.make_async_remote_copy(
            src_ref=held(way, k - 1, h, t),
            dst_ref=held(way, k, h, t),
            send_sem=send.at[way, k - 1, h],
            recv_sem=recv.at[way, k - 1, h],
            device_id=ways[way],
            device_id_type=MESH,
        )

    def pass_long(way, k, h):
        return pass_along(way, k, h, way, long_send, long_recv)

    def pass_short(way, k, h):
        return pass_along(way, k, h, 1 - way, short_send, short_recv)

    def takes(way, k):
        d = depth[way]
        return (d >= k) & ((k != 3) | (d <= NZ - 2))

    def gives(way, k):
        d = depth[way]
        return (d >= k - 1) & (d <= jnp.where(k == 3, NZ - 3, NZ - 2))

    def long_hop(way, k, h):
        there = held(way, k, h, way)
        pltpu.make_async_copy(there, there, long_recv.at[way, k - 1, h]).wait()

        @pl.when(k < 8)
        def _():
            pass_long(way, k + 1, h).start()

    def short_hop(way, k, h):
        @pl.when(takes(way, k))
        def _():
            there = held(way, k, h, 1 - way)
            pltpu.make_async_copy(there, there, short_recv.at[way, k - 1, h]).wait()

        @pl.when((k < 4) & gives(way, k + 1))
        def _():
            pass_short(way, k + 1, h).start()

    for way in (0, 1):
        for k in (1, 2, 4):
            @pl.when(jnp.logical_not(takes(way, k)))
            def _():
                slot = (BELOW, ABOVE)[way] + k
                for h in range(HEADS):
                    kv[slot, h, 1 - way] = jnp.zeros((ROWS, DIM), jnp.bfloat16)

    def first_hop(way, h, t, x, source):
        rows = pl.ds(pl.multiple_of(x * TOK, TOK), TOK)
        send, recv = (long_send, long_recv) if t == way else (short_send, short_recv)
        return pltpu.make_async_remote_copy(
            src_ref=source,
            dst_ref=held(way, 1, h, t).at[rows],
            send_sem=send.at[way, 0, h],
            recv_sem=recv.at[way, 0, h],
            device_id=ways[way],
            device_id_type=MESH,
        )

    def own_long(h):
        for way in (0, 1):
            first_hop(way, h, way, mx, piece(way, h, mx)).start()

    def own_short(h):
        for way in (0, 1):
            @pl.when(gives(way, 1))
            def _():
                first_hop(way, h, 1 - way, mx, piece(1 - way, h, mx)).start()

    def start_long(h):
        for d in (1, 3, 2):
            x = lax.rem(mx + NX - d, NX)
            for way in (0, 1):
                there = landing(way, h, x)
                pltpu.make_async_copy(there, there, in_recv.at[way, h, d - 1]).wait()
                first_hop(way, h, way, x, there).start()

    def start_short(h):
        for d in (1, 3, 2):
            x = lax.rem(mx + NX - d, NX)
            for way in (0, 1):
                @pl.when(gives(way, 1))
                def _():
                    first_hop(way, h, 1 - way, x, landing(1 - way, h, x)).start()

    staging[0].wait()
    staging[1].wait()
    send_pieces((0, 1), 0)
    over_heads(own_long)
    send_pieces((0, 1), 1)
    send_pieces((0, 1), 2)
    over_heads(own_short)
    over_heads(start_long)
    over_heads(start_short)
    staging[2].wait()
    over_heads(functools.partial(send_pieces, (2,)))

    def start_sibling(h):
        kept(0, h).wait()
        kept(1, h).wait()
        pass_on(OWN, SIB, h, sibling).start()

    over_heads(start_sibling)
    for copy in table:
        copy.wait()

    def bias_of(group):
        inside = (group >= 0) & (group < GROUPS)
        row = jnp.clip(group, 0, GROUPS - 1)
        count = jnp.where(inside, counts[0, row], 0)
        first, second = picks[0, row], picks[1, row]
        return [
            jnp.where(
                (group == me) | ((count > 0) & (first == j)) | ((count > 1) & (second == j)), 0.0, -HIDE
            )
            for j in (0, 1)
        ]

    def attend(h, parts):
        query = qs[h]
        raw, biases, highs = [], [], []
        for key_slot, _, group in parts:
            s = lax.dot_general(
                kv[key_slot, h, 0], query, (((1,), (1,)), ((), ())), preferred_element_type=jnp.float32
            )
            for j, bias in enumerate(bias_of(group)):
                block = s[j * BLOCK:(j + 1) * BLOCK]
                raw.append(block)
                biases.append(bias)
                highs.append(jnp.max(block, axis=0, keepdims=True) + bias)
        newest = functools.reduce(jnp.maximum, highs + [top[h]])
        rescale = jnp.exp2((top[h] - newest) * EXPONENT)
        row_sum = total[h] * rescale
        mixed = acc[h] * rescale
        for i, (_, value_slot, _) in enumerate(parts):
            weights = []
            for j in (2 * i, 2 * i + 1):
                w = jnp.exp2((raw[j] - (newest - biases[j])) * EXPONENT)
                weights.append(w.astype(jnp.bfloat16))
                row_sum = row_sum + jnp.sum(w.reshape(BLOCK // 8, 8, ROWS), axis=0)
            mixed = mixed + lax.dot_general(
                kv[value_slot, h, 1], jnp.concatenate(weights, axis=0),
                (((0,), (0,)), ((), ())), preferred_element_type=jnp.float32,
            )
        top[h] = newest
        total[h] = row_sum
        acc[h] = mixed

    top[...] = jnp.full(top.shape, -HIDE, jnp.float32)
    total[...] = jnp.zeros(total.shape, jnp.float32)
    acc[...] = jnp.zeros(acc.shape, jnp.float32)

    zstep = NY * NC
    own_pair = ((OWN, OWN, me), (SIB, SIB, me + 1 - 2 * core))
    far = lax.rem(me + 8 * zstep, GROUPS)
    sib2 = (SIB2, SIB2, me - 1 + 2 * core)
    opposite = (BELOW + 8, ABOVE + 8, far)

    def near(k):
        return (
            (BELOW + k, BELOW + k, me - k * zstep),
            (ABOVE + k, ABOVE + k, me + k * zstep),
        )

    two_pair = ((M2, M2, me - 2), (P2, P2, me + 2))
    four_pair = ((M4, M4, me - 4), (P4, P4, me + 4))
    pairs = {0: own_pair, 4: near(1), 6: two_pair, 7: near(2), 9: four_pair, 10: near(4)}
    singles = {8: sib2, 11: opposite}

    def chosen(stage, side):
        table = [pairs.get(i, own_pair)[side] for i in range(STAGES)]
        return tuple(pick(stage, [entry[field] for entry in table]) for field in range(3))

    def extras(stage, h):
        @pl.when(stage == 0)
        def _():
            arrived(2, h)
            await_slot(SIB, h)

        @pl.when(((stage == 0) & (my < NY - 1)) | ((stage == 3) & (my == NY - 1)))
        def _():
            pass_on(jnp.where(my == NY - 1, BELOW + 1, OWN), M2, h, right).start()

        @pl.when(((stage == 1) & (my > 0)) | ((stage == 3) & (my == 0)))
        def _():
            pass_on(jnp.where(my == 0, ABOVE + 1, OWN), P2, h, left).start()

        @pl.when((stage == 3) & (my == 2))
        def _():
            pass_on(BELOW + 1, VIA_M4, h, right).start()

        @pl.when((stage == 3) & (my == 1))
        def _():
            pass_on(ABOVE + 1, VIA_P4, h, left).start()

        @pl.when(stage == 6)
        def _():
            await_slot(M2, h)
            await_slot(P2, h)
            pass_on(jnp.where(core == 1, M2, P2), SIB2, h, sibling).start()

        @pl.when(stage == 7)
        def _():
            @pl.when(my == NY - 1)
            def _():
                await_slot(VIA_M4, h)

            @pl.when(my == 0)
            def _():
                await_slot(VIA_P4, h)

            pass_on(jnp.where(my == NY - 1, VIA_M4, M2), M4, h, right).start()
            pass_on(jnp.where(my == 0, VIA_P4, P2), P4, h, left).start()

        @pl.when(stage == 8)
        def _():
            await_slot(SIB2, h)
            for t in (0, 1, 2):
                for d in (1, 2, 3):
                    exchange(t, h, d).wait_send()
            release(h, (SIB, M2, P2), (1, 2, 3, 4), (1,))
            for slot, place in ((VIA_M4, 2), (VIA_P4, 1)):
                @pl.when(my == place)
                def _():
                    pass_on(OWN, slot, h, sibling).wait_send()

        @pl.when(stage == 9)
        def _():
            await_slot(M4, h)
            await_slot(P4, h)


    def release(h, slots, long_hops, short_hops):
        for slot in slots:
            pass_on(OWN, slot, h, sibling).wait_send()
        for way in (0, 1):
            for k in long_hops:
                pass_long(way, k, h).wait_send()
            for k in short_hops:
                @pl.when(gives(way, k))
                def _():
                    pass_short(way, k, h).wait_send()

    short_at = [
        [pick(mz, [orders[j] + j for orders in ORDER[way]]) for j in range(4)] for way in (0, 1)
    ]

    def one_stage(stage, carry):
        hops = []
        for way in (0, 1):
            is_short = functools.reduce(jnp.logical_or, [stage == at for at in short_at[way]])
            short = sum(jnp.where(stage == at, j, 0) for j, at in enumerate(short_at[way], 1))
            long = stage + 1 - sum(jnp.where(at < stage, 1, 0) for at in short_at[way])
            hops.append((is_short, short, long))
        attends = functools.reduce(jnp.logical_or, [stage == i for i in pairs])
        first, second = chosen(stage, 0), chosen(stage, 1)
        alone = functools.reduce(jnp.logical_or, [stage == i for i in singles])
        single = tuple(jnp.where(stage == 8, *entry) for entry in zip(sib2, opposite))

        def one_head(h):
            for way, (is_short, short, long) in enumerate(hops):
                @pl.when(is_short)
                def _():
                    short_hop(way, short, h)

                @pl.when(jnp.logical_not(is_short))
                def _():
                    long_hop(way, long, h)

            extras(stage, h)

            @pl.when(attends)
            def _():
                attend(h, [first, second])

            @pl.when(alone)
            def _():
                attend(h, [single])

            @pl.when(stage == STAGES - 1)
            def _():
                finish_head(h)

        over_heads(one_head)
        return carry

    def out_columns(x, h):
        return out_hbm.at[:, pl.ds(pl.multiple_of((x * HEADS + h) * DIM, DIM), DIM)]

    def out_rows(x, h):
        return os.at[h, pl.ds(pl.multiple_of(x * TOK, TOK), TOK), :]

    def give_back(h, d):
        target = lax.rem(mx + d, NX)
        return pltpu.make_async_remote_copy(
            src_ref=out_rows(target, h),
            dst_ref=out_columns(mx, h),
            send_sem=out_send.at[h, d - 1],
            recv_sem=out_recv.at[h, d - 1],
            device_id=(me, target),
            device_id_type=MESH,
        )

    def keep_back(h):
        return pltpu.make_async_copy(out_rows(mx, h), out_columns(mx, h), out_local.at[h])

    def finish_head(h):
        row_total = jnp.sum(total[h], axis=0, keepdims=True)
        os[h] = jnp.transpose(acc[h] / row_total).astype(jnp.bfloat16)
        for d in (2, 1, 3):
            give_back(h, d).start()
        keep_back(h).start()

    lax.fori_loop(0, STAGES, one_stage, 0)

    def finish(h):
        release(h, (M4, P4, SIB2), (5, 6, 7, 8), (2, 3, 4))
        for d in (1, 2, 3):
            give_back(h, d).wait_send()
        keep_back(h).wait()
        for d in (1, 2, 3):
            there = out_columns(lax.rem(mx + NX - d, NX), h)
            pltpu.make_async_copy(there, there, out_recv.at[h, d - 1]).wait()

    over_heads(finish)


def local(queries, keys, values, block_picks, block_counts):
    picks = jnp.transpose(block_picks, (0, 2, 1))
    dma = pltpu.SemaphoreType.DMA
    return pl.pallas_call(
        kernel,
        out_shape=jax.ShapeDtypeStruct(queries.shape, queries.dtype),
        in_specs=[pl.BlockSpec(memory_space=pltpu.HBM)] * 5,
        out_specs=pl.BlockSpec(memory_space=pl.ANY),
        scratch_shapes=[
            pltpu.VMEM((SLOTS, HEADS, 2, ROWS, DIM), jnp.bfloat16),
            pltpu.VMEM((3,) + queries.shape, jnp.bfloat16),
            pltpu.VMEM((HEADS, ROWS, DIM), jnp.bfloat16),
            pltpu.VMEM((HEADS, ROWS, DIM), jnp.bfloat16),
            pltpu.VMEM((HEADS, DIM, ROWS), jnp.float32),
            pltpu.VMEM((HEADS, 1, ROWS), jnp.float32),
            pltpu.VMEM((HEADS, 8, ROWS), jnp.float32),
            pltpu.SMEM((1, GROUPS), jnp.int32),
            pltpu.SMEM((2, GROUPS), jnp.int32),
            dma((3, HEADS, 3)), dma((3, HEADS, 3)), dma((3, HEADS)),
            dma((SLOTS - M2, HEADS)), dma((SLOTS - M2, HEADS)),
            dma((2, 8, HEADS)), dma((2, 8, HEADS)), dma((2, 4, HEADS)), dma((2, 4, HEADS)),
            dma((HEADS, 3)), dma((HEADS, 3)), dma((HEADS,)), dma((5,)),
        ],
        compiler_params=pltpu.CompilerParams(
            collective_id=0, has_side_effects=True, vmem_limit_bytes=32 * 1024 * 1024
        ),
        name="radial_attention",
    )(*(pltpu.with_memory_space_constraint(x, pltpu.HBM) for x in (queries, keys, values, picks, block_counts)))


def solution(mesh):
    placed = P(("frames", "heads"), None)
    return jax.shard_map(
        local,
        mesh=mesh,
        in_specs=(placed, placed, placed, P(), P()),
        out_specs=placed,
        check_vma=False,
    )
```

```python
import functools
import math

import jax
import jax.numpy as jnp
from jax import lax
from jax.experimental import pallas as pl
from jax.experimental.pallas import tpu as pltpu
from jax.sharding import PartitionSpec as P

MESH = pl.DeviceIdType.MESH

NZ, NY, NC, NX = 16, 4, 2, 4
GROUPS = NZ * NY * NC
HEADS = 3
DIM = 128
BLOCK = 128
TOK = 64
ROWS = TOK * NX
HIDE = 1e30
EXPONENT = math.log2(math.e) / math.sqrt(DIM)

OWN = 0
BELOW = 0
ABOVE = 8
M2, P2, M4, P4, SIB, SIB2, VIA_M4, VIA_P4 = 17, 18, 19, 20, 21, 22, 23, 24
SLOTS = 25

LONG = (0, 1, 2, 4, 6, 8)
SHORT = (0, 1, 2, 4)

STAGES = (
    ("long", 1), ("long", 2), ("short", 1), ("long", 3), ("short", 2), ("long", 4),
    ("none", 0), ("short", 3), ("none", 0), ("long", 5),
)


def pick(index, values):
    found = values[-1]
    for i, value in enumerate(values[:-1]):
        found = jnp.where(index == i, value, found)
    return found


def kernel(
    q_hbm, k_hbm, v_hbm, picks_hbm, counts_hbm, out_hbm,
    kv, staged, qs, os, acc, top, total, counts, picks,
    in_send, in_recv, in_local, kv_send, kv_recv, long_send, long_recv, short_send, short_recv,
    out_send, out_recv, out_local, small_sem, entered,
):
    me = lax.axis_index("frames")
    mx = lax.axis_index("heads")
    core = lax.rem(me, NC)
    my = lax.rem(me // NC, NY)
    mz = me // (NC * NY)

    def frame(z, y, c):
        return (z * NY + y) * NC + c

    def along(way, chips):
        z = mz + chips if way == 0 else mz + NZ - chips
        return (frame(lax.rem(z, NZ), my, core), mx)

    right = (frame(mz, lax.rem(my + 1, NY), core), mx)
    left = (frame(mz, lax.rem(my + NY - 1, NY), core), mx)
    sibling = (frame(mz, my, 1 - core), mx)
    others = [(me, lax.rem(mx + d, NX)) for d in (1, 2, 3)]

    table = [
        pltpu.make_async_copy(counts_hbm.at[pl.ds(me, 1)], counts, small_sem.at[0]),
        pltpu.make_async_copy(picks_hbm.at[me], picks, small_sem.at[1]),
    ]
    staging = [
        pltpu.make_async_copy(source, staged.at[t], small_sem.at[2 + t])
        for t, source in enumerate((k_hbm, v_hbm, q_hbm))
    ]
    for copy in staging + table:
        copy.start()

    barrier = pltpu.get_barrier_semaphore()
    partners = [along(0, 1), along(1, 1), right, left, sibling] + others
    for partner in partners:
        pl.semaphore_signal(barrier, inc=1, device_id=partner, device_id_type=MESH)
    pl.semaphore_wait(barrier, len(partners))

    for way in (0, 1):
        pl.semaphore_signal(entered.at[way], inc=1, device_id=along(1 - way, 1), device_id_type=MESH)

    def landing(t, h, x):
        rows = pl.ds(pl.multiple_of(x * TOK, TOK), TOK)
        if t == 2:
            return qs.at[h, rows, :]
        return kv.at[OWN, h, t, rows, :]

    def piece(t, h, x):
        return staged.at[t, :, pl.ds(pl.multiple_of((x * HEADS + h) * DIM, DIM), DIM)]

    def exchange(t, h, d):
        target = lax.rem(mx + d, NX)
        return pltpu.make_async_remote_copy(
            src_ref=piece(t, h, target),
            dst_ref=landing(t, h, mx),
            send_sem=in_send.at[t, h, d - 1],
            recv_sem=in_recv.at[t, h, d - 1],
            device_id=(me, target),
            device_id_type=MESH,
        )

    def kept(t, h):
        return pltpu.make_async_copy(piece(t, h, mx), landing(t, h, mx), in_local.at[t, h])

    def arrived(t, h):
        kept(t, h).wait()
        for d in (1, 2, 3):
            source = lax.rem(mx + NX - d, NX)
            there = landing(t, h, source)
            pltpu.make_async_copy(there, there, in_recv.at[t, h, d - 1]).wait()

    def over_heads(body):
        def step(h, carry):
            body(h)
            return carry

        lax.fori_loop(0, HEADS, step, 0)

    def send_pieces(tensors, h):
        for t in tensors:
            for d in (2, 1, 3):
                exchange(t, h, d).start()
            kept(t, h).start()

    def pass_on(source, slot, h, target):
        return pltpu.make_async_remote_copy(
            src_ref=kv.at[source, h],
            dst_ref=kv.at[slot, h],
            send_sem=kv_send.at[slot - M2, h],
            recv_sem=kv_recv.at[slot - M2, h],
            device_id=target,
            device_id_type=MESH,
        )

    def await_slot(slot, h):
        there = kv.at[slot, h]
        pltpu.make_async_copy(there, there, kv_recv.at[slot - M2, h]).wait()

    depth = (mz, NZ - 1 - mz)

    def held(way, reach, h, t):
        return kv.at[jnp.where(reach == 0, OWN, (BELOW, ABOVE)[way] + reach), h, t]

    def pass_along(way, s, h, t, reaches, send, recv):
        start, end = pick(s, (0,) + reaches[:-1]), pick(s, reaches)
        return pltpu.make_async_remote_copy(
            src_ref=held(way, start, h, t),
            dst_ref=held(way, end, h, t),
            send_sem=send.at[way, s - 1, h],
            recv_sem=recv.at[way, s - 1, h],
            device_id=along(way, end - start),
            device_id_type=MESH,
        )

    def pass_long(way, s, h):
        return pass_along(way, s, h, way, LONG, long_send, long_recv)

    def pass_short(way, s, h):
        return pass_along(way, s, h, 1 - way, SHORT, short_send, short_recv)

    def takes(way, s):
        return depth[way] >= pick(s, SHORT)

    def gives(way, s):
        start, end = pick(s, (0,) + SHORT[:-1]), pick(s, SHORT)
        return (depth[way] >= start) & (depth[way] < NZ - (end - start))

    def long_hop(s, h):
        for way in (0, 1):
            there = held(way, pick(s, LONG), h, way)
            pltpu.make_async_copy(there, there, long_recv.at[way, s - 1, h]).wait()

            @pl.when(s < len(LONG) - 1)
            def _():
                pass_long(way, s + 1, h).start()

    def short_hop(s, h):
        for way in (0, 1):
            @pl.when(takes(way, s))
            def _():
                there = held(way, pick(s, SHORT), h, 1 - way)
                pltpu.make_async_copy(there, there, short_recv.at[way, s - 1, h]).wait()

            @pl.when((s < len(SHORT) - 1) & gives(way, s + 1))
            def _():
                pass_short(way, s + 1, h).start()

    for way in (0, 1):
        for s, reach in enumerate(SHORT[1:], 1):
            @pl.when(jnp.logical_not(takes(way, s)))
            def _():
                slot = (BELOW, ABOVE)[way] + reach
                for h in range(HEADS):
                    kv[slot, h, 1 - way] = jnp.zeros((ROWS, DIM), jnp.bfloat16)

    def first_hop(way, h, t, x, source):
        rows = pl.ds(pl.multiple_of(x * TOK, TOK), TOK)
        send, recv = (long_send, long_recv) if t == way else (short_send, short_recv)
        return pltpu.make_async_remote_copy(
            src_ref=source,
            dst_ref=held(way, 1, h, t).at[rows],
            send_sem=send.at[way, 0, h],
            recv_sem=recv.at[way, 0, h],
            device_id=along(way, 1),
            device_id_type=MESH,
        )

    def own_long(h):
        for way in (0, 1):
            first_hop(way, h, way, mx, piece(way, h, mx)).start()

    def own_short(h):
        for way in (0, 1):
            @pl.when(gives(way, 1))
            def _():
                first_hop(way, h, 1 - way, mx, piece(1 - way, h, mx)).start()

    def start_long(h):
        for d in (1, 3, 2):
            x = lax.rem(mx + NX - d, NX)
            for way in (0, 1):
                there = landing(way, h, x)
                pltpu.make_async_copy(there, there, in_recv.at[way, h, d - 1]).wait()
                first_hop(way, h, way, x, there).start()

    def start_short(h):
        for d in (1, 3, 2):
            x = lax.rem(mx + NX - d, NX)
            for way in (0, 1):
                @pl.when(gives(way, 1))
                def _():
                    first_hop(way, h, 1 - way, x, landing(1 - way, h, x)).start()

    staging[0].wait()
    staging[1].wait()
    send_pieces((0, 1), 0)
    over_heads(own_long)
    send_pieces((0, 1), 1)
    send_pieces((0, 1), 2)
    over_heads(own_short)
    over_heads(start_long)
    over_heads(start_short)
    staging[2].wait()
    over_heads(functools.partial(send_pieces, (2,)))

    def start_sibling(h):
        kept(0, h).wait()
        kept(1, h).wait()
        pass_on(OWN, SIB, h, sibling).start()

    over_heads(start_sibling)
    for way in (0, 1):
        pl.semaphore_wait(entered.at[way], 1)
    for copy in table:
        copy.wait()

    def bias_of(group):
        inside = (group >= 0) & (group < GROUPS)
        row = jnp.clip(group, 0, GROUPS - 1)
        count = jnp.where(inside, counts[0, row], 0)
        first, second = picks[0, row], picks[1, row]
        return [
            jnp.where(
                (group == me) | ((count > 0) & (first == j)) | ((count > 1) & (second == j)), 0.0, -HIDE
            )
            for j in (0, 1)
        ]

    def attend(h, parts):
        query = qs[h]
        raw, biases, highs = [], [], []
        for key_slot, _, group in parts:
            s = lax.dot_general(
                kv[key_slot, h, 0], query, (((1,), (1,)), ((), ())), preferred_element_type=jnp.float32
            )
            for j, bias in enumerate(bias_of(group)):
                block = s[j * BLOCK:(j + 1) * BLOCK]
                raw.append(block)
                biases.append(bias)
                highs.append(jnp.max(block, axis=0, keepdims=True) + bias)
        newest = functools.reduce(jnp.maximum, highs + [top[h]])
        rescale = jnp.exp2((top[h] - newest) * EXPONENT)
        row_sum = total[h] * rescale
        mixed = acc[h] * rescale
        for i, (_, value_slot, _) in enumerate(parts):
            weights = []
            for j in (2 * i, 2 * i + 1):
                w = jnp.exp2((raw[j] - (newest - biases[j])) * EXPONENT)
                weights.append(w.astype(jnp.bfloat16))
                row_sum = row_sum + jnp.sum(w.reshape(BLOCK // 8, 8, ROWS), axis=0)
            mixed = mixed + lax.dot_general(
                kv[value_slot, h, 1], jnp.concatenate(weights, axis=0),
                (((0,), (0,)), ((), ())), preferred_element_type=jnp.float32,
            )
        top[h] = newest
        total[h] = row_sum
        acc[h] = mixed

    top[...] = jnp.full(top.shape, -HIDE, jnp.float32)
    total[...] = jnp.zeros(total.shape, jnp.float32)
    acc[...] = jnp.zeros(acc.shape, jnp.float32)

    zstep = NY * NC
    own_pair = ((OWN, OWN, me), (SIB, SIB, me + 1 - 2 * core))
    far = lax.rem(me + 8 * zstep, GROUPS)
    sib2 = (SIB2, SIB2, me - 1 + 2 * core)
    opposite = (BELOW + 8, ABOVE + 8, far)

    def near(k):
        return (
            (BELOW + k, BELOW + k, me - k * zstep),
            (ABOVE + k, ABOVE + k, me + k * zstep),
        )

    two_pair = ((M2, M2, me - 2), (P2, P2, me + 2))
    four_pair = ((M4, M4, me - 4), (P4, P4, me + 4))
    pairs = {0: own_pair, 2: near(1), 4: two_pair, 5: near(2), 6: four_pair, 7: near(4)}
    singles = {8: sib2, 9: opposite}

    def chosen(stage, side):
        table = [pairs.get(i, own_pair)[side] for i in range(len(STAGES))]
        return tuple(pick(stage, [entry[field] for entry in table]) for field in range(3))

    def extras(stage, h):
        @pl.when(stage == 0)
        def _():
            arrived(2, h)
            await_slot(SIB, h)

        @pl.when(((stage == 0) & (my < NY - 1)) | ((stage == 2) & (my == NY - 1)))
        def _():
            pass_on(jnp.where(my == NY - 1, BELOW + 1, OWN), M2, h, right).start()

        @pl.when(((stage == 1) & (my > 0)) | ((stage == 2) & (my == 0)))
        def _():
            pass_on(jnp.where(my == 0, ABOVE + 1, OWN), P2, h, left).start()

        @pl.when((stage == 2) & (my == 2))
        def _():
            pass_on(BELOW + 1, VIA_M4, h, right).start()

        @pl.when((stage == 2) & (my == 1))
        def _():
            pass_on(ABOVE + 1, VIA_P4, h, left).start()

        @pl.when(stage == 4)
        def _():
            await_slot(M2, h)
            await_slot(P2, h)
            pass_on(jnp.where(core == 1, M2, P2), SIB2, h, sibling).start()

            @pl.when(my == NY - 1)
            def _():
                await_slot(VIA_M4, h)

            @pl.when(my == 0)
            def _():
                await_slot(VIA_P4, h)

            pass_on(jnp.where(my == NY - 1, VIA_M4, M2), M4, h, right).start()
            pass_on(jnp.where(my == 0, VIA_P4, P2), P4, h, left).start()

        @pl.when(stage == 8)
        def _():
            await_slot(SIB2, h)
            for t in (0, 1, 2):
                for d in (1, 2, 3):
                    exchange(t, h, d).wait_send()
            release(h, (SIB, M2, P2), (1, 2, 3), (1, 2))
            for slot, place in ((VIA_M4, 2), (VIA_P4, 1)):
                @pl.when(my == place)
                def _():
                    pass_on(OWN, slot, h, sibling).wait_send()

        @pl.when(stage == 6)
        def _():
            await_slot(M4, h)
            await_slot(P4, h)


    def release(h, slots, long_hops, short_hops):
        for slot in slots:
            pass_on(OWN, slot, h, sibling).wait_send()
        for way in (0, 1):
            for k in long_hops:
                pass_long(way, k, h).wait_send()
            for k in short_hops:
                @pl.when(gives(way, k))
                def _():
                    pass_short(way, k, h).wait_send()

    def one_stage(stage, carry):
        hop = pick(stage, [k for _, k in STAGES])
        is_long = functools.reduce(
            jnp.logical_or, [stage == i for i, (kind, _) in enumerate(STAGES) if kind == "long"]
        )
        is_short = functools.reduce(
            jnp.logical_or, [stage == i for i, (kind, _) in enumerate(STAGES) if kind == "short"]
        )
        attends = functools.reduce(jnp.logical_or, [stage == i for i in pairs])
        first, second = chosen(stage, 0), chosen(stage, 1)
        alone = functools.reduce(jnp.logical_or, [stage == i for i in singles])
        single = tuple(jnp.where(stage == 8, *entry) for entry in zip(sib2, opposite))

        def one_head(h):
            @pl.when(is_long)
            def _():
                long_hop(hop, h)

            @pl.when(is_short)
            def _():
                short_hop(hop, h)

            extras(stage, h)

            @pl.when(attends)
            def _():
                attend(h, [first, second])

            @pl.when(alone)
            def _():
                attend(h, [single])

            @pl.when(stage == len(STAGES) - 1)
            def _():
                finish_head(h)

        over_heads(one_head)
        return carry

    def out_columns(x, h):
        return out_hbm.at[:, pl.ds(pl.multiple_of((x * HEADS + h) * DIM, DIM), DIM)]

    def out_rows(x, h):
        return os.at[h, pl.ds(pl.multiple_of(x * TOK, TOK), TOK), :]

    def give_back(h, d):
        target = lax.rem(mx + d, NX)
        return pltpu.make_async_remote_copy(
            src_ref=out_rows(target, h),
            dst_ref=out_columns(mx, h),
            send_sem=out_send.at[h, d - 1],
            recv_sem=out_recv.at[h, d - 1],
            device_id=(me, target),
            device_id_type=MESH,
        )

    def keep_back(h):
        return pltpu.make_async_copy(out_rows(mx, h), out_columns(mx, h), out_local.at[h])

    def finish_head(h):
        row_total = jnp.sum(total[h], axis=0, keepdims=True)
        os[h] = jnp.transpose(acc[h] / row_total).astype(jnp.bfloat16)
        for d in (2, 1, 3):
            give_back(h, d).start()
        keep_back(h).start()

    lax.fori_loop(0, len(STAGES), one_stage, 0)

    def finish(h):
        release(h, (M4, P4, SIB2), (4, 5), (3,))
        for d in (1, 2, 3):
            give_back(h, d).wait_send()
        keep_back(h).wait()
        for d in (1, 2, 3):
            there = out_columns(lax.rem(mx + NX - d, NX), h)
            pltpu.make_async_copy(there, there, out_recv.at[h, d - 1]).wait()

    over_heads(finish)


def local(queries, keys, values, block_picks, block_counts):
    picks = jnp.transpose(block_picks, (0, 2, 1))
    dma = pltpu.SemaphoreType.DMA
    return pl.pallas_call(
        kernel,
        out_shape=jax.ShapeDtypeStruct(queries.shape, queries.dtype),
        in_specs=[pl.BlockSpec(memory_space=pltpu.HBM)] * 5,
        out_specs=pl.BlockSpec(memory_space=pl.ANY),
        scratch_shapes=[
            pltpu.VMEM((SLOTS, HEADS, 2, ROWS, DIM), jnp.bfloat16),
            pltpu.VMEM((3,) + queries.shape, jnp.bfloat16),
            pltpu.VMEM((HEADS, ROWS, DIM), jnp.bfloat16),
            pltpu.VMEM((HEADS, ROWS, DIM), jnp.bfloat16),
            pltpu.VMEM((HEADS, DIM, ROWS), jnp.float32),
            pltpu.VMEM((HEADS, 1, ROWS), jnp.float32),
            pltpu.VMEM((HEADS, 8, ROWS), jnp.float32),
            pltpu.SMEM((1, GROUPS), jnp.int32),
            pltpu.SMEM((2, GROUPS), jnp.int32),
            dma((3, HEADS, 3)), dma((3, HEADS, 3)), dma((3, HEADS)),
            dma((SLOTS - M2, HEADS)), dma((SLOTS - M2, HEADS)),
            dma((2, 5, HEADS)), dma((2, 5, HEADS)), dma((2, 3, HEADS)), dma((2, 3, HEADS)),
            dma((HEADS, 3)), dma((HEADS, 3)), dma((HEADS,)), dma((5,)), pltpu.SemaphoreType.REGULAR((2,)),
        ],
        compiler_params=pltpu.CompilerParams(
            collective_id=0, has_side_effects=True, vmem_limit_bytes=32 * 1024 * 1024
        ),
        name="radial_attention",
    )(*(pltpu.with_memory_space_constraint(x, pltpu.HBM) for x in (queries, keys, values, picks, block_counts)))


def solution(mesh):
    placed = P(("frames", "heads"), None)
    return jax.shard_map(
        local,
        mesh=mesh,
        in_specs=(placed, placed, placed, P(), P()),
        out_specs=placed,
        check_vma=False,
    )
```

```python
import functools
import math

import jax
import jax.numpy as jnp
from jax import lax
from jax.experimental import pallas as pl
from jax.experimental.pallas import tpu as pltpu
from jax.sharding import PartitionSpec as P

MESH = pl.DeviceIdType.MESH

NZ, NY, NC, NX = 16, 4, 2, 4
GROUPS = NZ * NY * NC
HEADS = 3
DIM = 128
BLOCK = 128
TOK = 64
ROWS = TOK * NX
HIDE = 1e30
EXPONENT = math.log2(math.e) / math.sqrt(DIM)

OWN = 0
BELOW = 0
ABOVE = 8
M2, P2, M4, P4, SIB, SIB2, VIA_M4, VIA_P4 = 17, 18, 19, 20, 21, 22, 23, 24
SLOTS = 25

LONG = ((0, 1, 2, 4, 6, 8), (0, 1, 2, 3, 4, 5, 6, 7, 8))
SHORT = ((0, 1, 2, 4), (0, 1, 2, 3, 4))

STAGES = (
    (
        ("long", 1), ("long", 2), ("short", 1), ("long", 3), ("short", 2), ("long", 4),
        ("none", 0), ("short", 3), ("none", 0), ("long", 5), ("none", 0), ("none", 0),
    ),
    (
        ("long", 1), ("long", 2), ("long", 3), ("short", 1), ("long", 4), ("long", 5),
        ("short", 2), ("long", 6), ("short", 3), ("long", 7), ("short", 4), ("long", 8),
    ),
)
COUNT = 12


def pick(index, values):
    found = values[-1]
    for i, value in enumerate(values[:-1]):
        found = jnp.where(index == i, value, found)
    return found


def kernel(
    q_hbm, k_hbm, v_hbm, picks_hbm, counts_hbm, out_hbm,
    kv, staged, qs, os, acc, top, total, counts, picks,
    in_send, in_recv, in_local, kv_send, kv_recv, long_send, long_recv, short_send, short_recv,
    out_send, out_recv, out_local, small_sem, entered,
):
    me = lax.axis_index("frames")
    mx = lax.axis_index("heads")
    core = lax.rem(me, NC)
    my = lax.rem(me // NC, NY)
    mz = me // (NC * NY)

    def frame(z, y, c):
        return (z * NY + y) * NC + c

    def along(way, chips):
        z = mz + chips if way == 0 else mz + NZ - chips
        return (frame(lax.rem(z, NZ), my, core), mx)

    right = (frame(mz, lax.rem(my + 1, NY), core), mx)
    left = (frame(mz, lax.rem(my + NY - 1, NY), core), mx)
    sibling = (frame(mz, my, 1 - core), mx)
    others = [(me, lax.rem(mx + d, NX)) for d in (1, 2, 3)]

    table = [
        pltpu.make_async_copy(counts_hbm.at[pl.ds(me, 1)], counts, small_sem.at[0]),
        pltpu.make_async_copy(picks_hbm.at[me], picks, small_sem.at[1]),
    ]
    staging = [
        pltpu.make_async_copy(source, staged.at[t], small_sem.at[2 + t])
        for t, source in enumerate((k_hbm, v_hbm, q_hbm))
    ]
    for copy in staging + table:
        copy.start()

    barrier = pltpu.get_barrier_semaphore()
    partners = [along(0, 1), along(1, 1), right, left, sibling] + others
    for partner in partners:
        pl.semaphore_signal(barrier, inc=1, device_id=partner, device_id_type=MESH)
    pl.semaphore_wait(barrier, len(partners))

    for way in (0, 1):
        pl.semaphore_signal(entered.at[way], inc=1, device_id=along(1 - way, 1), device_id_type=MESH)

    def landing(t, h, x):
        rows = pl.ds(pl.multiple_of(x * TOK, TOK), TOK)
        if t == 2:
            return qs.at[h, rows, :]
        return kv.at[OWN, h, t, rows, :]

    def piece(t, h, x):
        return staged.at[t, :, pl.ds(pl.multiple_of((x * HEADS + h) * DIM, DIM), DIM)]

    def exchange(t, h, d):
        target = lax.rem(mx + d, NX)
        return pltpu.make_async_remote_copy(
            src_ref=piece(t, h, target),
            dst_ref=landing(t, h, mx),
            send_sem=in_send.at[t, h, d - 1],
            recv_sem=in_recv.at[t, h, d - 1],
            device_id=(me, target),
            device_id_type=MESH,
        )

    def kept(t, h):
        return pltpu.make_async_copy(piece(t, h, mx), landing(t, h, mx), in_local.at[t, h])

    def arrived(t, h):
        kept(t, h).wait()
        for d in (1, 2, 3):
            source = lax.rem(mx + NX - d, NX)
            there = landing(t, h, source)
            pltpu.make_async_copy(there, there, in_recv.at[t, h, d - 1]).wait()

    def over_heads(body):
        def step(h, carry):
            body(h)
            return carry

        lax.fori_loop(0, HEADS, step, 0)

    def send_pieces(tensors, h):
        for t in tensors:
            for d in (2, 1, 3):
                exchange(t, h, d).start()
            kept(t, h).start()

    def pass_on(source, slot, h, target):
        return pltpu.make_async_remote_copy(
            src_ref=kv.at[source, h],
            dst_ref=kv.at[slot, h],
            send_sem=kv_send.at[slot - M2, h],
            recv_sem=kv_recv.at[slot - M2, h],
            device_id=target,
            device_id_type=MESH,
        )

    def await_slot(slot, h):
        there = kv.at[slot, h]
        pltpu.make_async_copy(there, there, kv_recv.at[slot - M2, h]).wait()

    depth = (mz, NZ - 1 - mz)

    def held(way, reach, h, t):
        return kv.at[jnp.where(reach == 0, OWN, (BELOW, ABOVE)[way] + reach), h, t]

    def by_core(zero, one):
        return jnp.where(core == 0, zero, one)

    def reach_of(s, reaches):
        return by_core(pick(s, reaches[0]), pick(s, reaches[1]))

    last_long, last_short = (by_core(len(r[0]) - 1, len(r[1]) - 1) for r in (LONG, SHORT))

    def pass_along(way, s, h, t, reaches, send, recv):
        start, end = reach_of(s - 1, reaches), reach_of(s, reaches)
        return pltpu.make_async_remote_copy(
            src_ref=held(way, start, h, t),
            dst_ref=held(way, end, h, t),
            send_sem=send.at[way, s - 1, h],
            recv_sem=recv.at[way, s - 1, h],
            device_id=along(way, end - start),
            device_id_type=MESH,
        )

    def pass_long(way, s, h):
        return pass_along(way, s, h, way, LONG, long_send, long_recv)

    def pass_short(way, s, h):
        return pass_along(way, s, h, 1 - way, SHORT, short_send, short_recv)

    def takes(way, s):
        d, reach = depth[way], reach_of(s, SHORT)
        return (s <= last_short) & (d >= reach) & ((reach != 3) | (d < NZ - 1))

    def gives(way, s):
        d, start, end = depth[way], reach_of(s - 1, SHORT), reach_of(s, SHORT)
        return (s <= last_short) & (d >= start) & (d < NZ - (end - start) - jnp.where(end == 3, 1, 0))

    def long_hop(s, h):
        for way in (0, 1):
            there = held(way, reach_of(s, LONG), h, way)
            pltpu.make_async_copy(there, there, long_recv.at[way, s - 1, h]).wait()

            @pl.when(s < last_long)
            def _():
                pass_long(way, s + 1, h).start()

    def short_hop(s, h):
        for way in (0, 1):
            @pl.when(takes(way, s))
            def _():
                there = held(way, reach_of(s, SHORT), h, 1 - way)
                pltpu.make_async_copy(there, there, short_recv.at[way, s - 1, h]).wait()

            @pl.when(gives(way, s + 1))
            def _():
                pass_short(way, s + 1, h).start()

    for way in (0, 1):
        for reach in (1, 2, 4):
            @pl.when(depth[way] < reach)
            def _():
                slot = (BELOW, ABOVE)[way] + reach
                for h in range(HEADS):
                    kv[slot, h, 1 - way] = jnp.zeros((ROWS, DIM), jnp.bfloat16)

    def first_hop(way, h, t, x, source):
        rows = pl.ds(pl.multiple_of(x * TOK, TOK), TOK)
        send, recv = (long_send, long_recv) if t == way else (short_send, short_recv)
        return pltpu.make_async_remote_copy(
            src_ref=source,
            dst_ref=held(way, 1, h, t).at[rows],
            send_sem=send.at[way, 0, h],
            recv_sem=recv.at[way, 0, h],
            device_id=along(way, 1),
            device_id_type=MESH,
        )

    def own_long(h):
        for way in (0, 1):
            first_hop(way, h, way, mx, piece(way, h, mx)).start()

    def own_short(h):
        for way in (0, 1):
            @pl.when(gives(way, 1))
            def _():
                first_hop(way, h, 1 - way, mx, piece(1 - way, h, mx)).start()

    def start_long(h):
        for d in (1, 3, 2):
            x = lax.rem(mx + NX - d, NX)
            for way in (0, 1):
                there = landing(way, h, x)
                pltpu.make_async_copy(there, there, in_recv.at[way, h, d - 1]).wait()
                first_hop(way, h, way, x, there).start()

    def start_short(h):
        for d in (1, 3, 2):
            x = lax.rem(mx + NX - d, NX)
            for way in (0, 1):
                @pl.when(gives(way, 1))
                def _():
                    first_hop(way, h, 1 - way, x, landing(1 - way, h, x)).start()

    staging[0].wait()
    staging[1].wait()
    send_pieces((0, 1), 0)
    over_heads(own_long)
    send_pieces((0, 1), 1)
    send_pieces((0, 1), 2)
    over_heads(own_short)
    over_heads(start_long)
    over_heads(start_short)
    staging[2].wait()
    over_heads(functools.partial(send_pieces, (2,)))

    def start_sibling(h):
        kept(0, h).wait()
        kept(1, h).wait()
        pass_on(OWN, SIB, h, sibling).start()

    over_heads(start_sibling)
    for way in (0, 1):
        pl.semaphore_wait(entered.at[way], 1)
    for copy in table:
        copy.wait()

    def bias_of(group):
        inside = (group >= 0) & (group < GROUPS)
        row = jnp.clip(group, 0, GROUPS - 1)
        count = jnp.where(inside, counts[0, row], 0)
        first, second = picks[0, row], picks[1, row]
        return [
            jnp.where(
                (group == me) | ((count > 0) & (first == j)) | ((count > 1) & (second == j)), 0.0, -HIDE
            )
            for j in (0, 1)
        ]

    def attend(h, parts):
        query = qs[h]
        raw, biases, highs = [], [], []
        for key_slot, _, group in parts:
            s = lax.dot_general(
                kv[key_slot, h, 0], query, (((1,), (1,)), ((), ())), preferred_element_type=jnp.float32
            )
            for j, bias in enumerate(bias_of(group)):
                block = s[j * BLOCK:(j + 1) * BLOCK]
                raw.append(block)
                biases.append(bias)
                highs.append(jnp.max(block, axis=0, keepdims=True) + bias)
        newest = functools.reduce(jnp.maximum, highs + [top[h]])
        rescale = jnp.exp2((top[h] - newest) * EXPONENT)
        row_sum = total[h] * rescale
        mixed = acc[h] * rescale
        for i, (_, value_slot, _) in enumerate(parts):
            weights = []
            for j in (2 * i, 2 * i + 1):
                w = jnp.exp2((raw[j] - (newest - biases[j])) * EXPONENT)
                weights.append(w.astype(jnp.bfloat16))
                row_sum = row_sum + jnp.sum(w.reshape(BLOCK // 8, 8, ROWS), axis=0)
            mixed = mixed + lax.dot_general(
                kv[value_slot, h, 1], jnp.concatenate(weights, axis=0),
                (((0,), (0,)), ((), ())), preferred_element_type=jnp.float32,
            )
        top[h] = newest
        total[h] = row_sum
        acc[h] = mixed

    top[...] = jnp.full(top.shape, -HIDE, jnp.float32)
    total[...] = jnp.zeros(total.shape, jnp.float32)
    acc[...] = jnp.zeros(acc.shape, jnp.float32)

    zstep = NY * NC
    own_pair = ((OWN, OWN, me), (SIB, SIB, me + 1 - 2 * core))
    far = lax.rem(me + 8 * zstep, GROUPS)
    sib2 = (SIB2, SIB2, me - 1 + 2 * core)
    opposite = (BELOW + 8, ABOVE + 8, far)

    def near(k):
        return (
            (BELOW + k, BELOW + k, me - k * zstep),
            (ABOVE + k, ABOVE + k, me + k * zstep),
        )

    two_pair = ((M2, M2, me - 2), (P2, P2, me + 2))
    four_pair = ((M4, M4, me - 4), (P4, P4, me + 4))
    pairs = [
        (by_core(*at), pair) for at, pair in (
            ((0, 0), own_pair), ((2, 4), near(1)), ((4, 6), two_pair),
            ((5, 7), near(2)), ((6, 9), four_pair), ((7, 10), near(4)),
        )
    ]
    far_stage = by_core(9, 11)

    def chosen(stage, side):
        found = own_pair[side]
        for at, pair in pairs[1:]:
            found = tuple(jnp.where(stage == at, new, old) for new, old in zip(pair[side], found))
        return found

    def extras(stage, h):
        @pl.when(stage == 0)
        def _():
            arrived(2, h)
            await_slot(SIB, h)

        @pl.when(((stage == 0) & (my < NY - 1)) | ((stage == by_core(2, 3)) & (my == NY - 1)))
        def _():
            pass_on(jnp.where(my == NY - 1, BELOW + 1, OWN), M2, h, right).start()

        @pl.when(((stage == 1) & (my > 0)) | ((stage == by_core(2, 3)) & (my == 0)))
        def _():
            pass_on(jnp.where(my == 0, ABOVE + 1, OWN), P2, h, left).start()

        @pl.when((stage == by_core(2, 3)) & (my == 2))
        def _():
            pass_on(BELOW + 1, VIA_M4, h, right).start()

        @pl.when((stage == by_core(2, 3)) & (my == 1))
        def _():
            pass_on(ABOVE + 1, VIA_P4, h, left).start()

        @pl.when(stage == by_core(4, 6))
        def _():
            await_slot(M2, h)
            await_slot(P2, h)
            pass_on(jnp.where(core == 1, M2, P2), SIB2, h, sibling).start()

            @pl.when(my == NY - 1)
            def _():
                await_slot(VIA_M4, h)

            @pl.when(my == 0)
            def _():
                await_slot(VIA_P4, h)

            pass_on(jnp.where(my == NY - 1, VIA_M4, M2), M4, h, right).start()
            pass_on(jnp.where(my == 0, VIA_P4, P2), P4, h, left).start()

        @pl.when(stage == 8)
        def _():
            await_slot(SIB2, h)
            for t in (0, 1, 2):
                for d in (1, 2, 3):
                    exchange(t, h, d).wait_send()
            release(h, (SIB, M2, P2), (1, 2, 3), (1, 2))
            for slot, place in ((VIA_M4, 2), (VIA_P4, 1)):
                @pl.when(my == place)
                def _():
                    pass_on(OWN, slot, h, sibling).wait_send()

        @pl.when(stage == by_core(6, 9))
        def _():
            await_slot(M4, h)
            await_slot(P4, h)


    def release(h, slots, long_hops, short_hops):
        for slot in slots:
            pass_on(OWN, slot, h, sibling).wait_send()
        for way in (0, 1):
            for k in long_hops:
                @pl.when(k <= last_long)
                def _():
                    pass_long(way, k, h).wait_send()

            for k in short_hops:
                @pl.when(gives(way, k))
                def _():
                    pass_short(way, k, h).wait_send()

    def one_stage(stage, carry):
        def is_kind(name):
            return by_core(*(
                functools.reduce(
                    jnp.logical_or, [stage == i for i, (kind, _) in enumerate(stages) if kind == name]
                )
                for stages in STAGES
            ))

        hop = by_core(*(pick(stage, [s for _, s in stages]) for stages in STAGES))
        is_long, is_short = is_kind("long"), is_kind("short")
        attends = functools.reduce(jnp.logical_or, [stage == at for at, _ in pairs])
        first, second = chosen(stage, 0), chosen(stage, 1)
        alone = (stage == 8) | (stage == far_stage)
        single = tuple(jnp.where(stage == 8, *entry) for entry in zip(sib2, opposite))

        def one_head(h):
            @pl.when(is_long)
            def _():
                long_hop(hop, h)

            @pl.when(is_short)
            def _():
                short_hop(hop, h)

            extras(stage, h)

            @pl.when(attends)
            def _():
                attend(h, [first, second])

            @pl.when(alone)
            def _():
                attend(h, [single])

            @pl.when(stage == far_stage)
            def _():
                finish_head(h)

        over_heads(one_head)
        return carry

    def out_columns(x, h):
        return out_hbm.at[:, pl.ds(pl.multiple_of((x * HEADS + h) * DIM, DIM), DIM)]

    def out_rows(x, h):
        return os.at[h, pl.ds(pl.multiple_of(x * TOK, TOK), TOK), :]

    def give_back(h, d):
        target = lax.rem(mx + d, NX)
        return pltpu.make_async_remote_copy(
            src_ref=out_rows(target, h),
            dst_ref=out_columns(mx, h),
            send_sem=out_send.at[h, d - 1],
            recv_sem=out_recv.at[h, d - 1],
            device_id=(me, target),
            device_id_type=MESH,
        )

    def keep_back(h):
        return pltpu.make_async_copy(out_rows(mx, h), out_columns(mx, h), out_local.at[h])

    def finish_head(h):
        row_total = jnp.sum(total[h], axis=0, keepdims=True)
        os[h] = jnp.transpose(acc[h] / row_total).astype(jnp.bfloat16)
        for d in (2, 1, 3):
            give_back(h, d).start()
        keep_back(h).start()

    lax.fori_loop(0, COUNT, one_stage, 0)

    def finish(h):
        release(h, (M4, P4, SIB2), (4, 5, 6, 7, 8), (3, 4))
        for d in (1, 2, 3):
            give_back(h, d).wait_send()
        keep_back(h).wait()
        for d in (1, 2, 3):
            there = out_columns(lax.rem(mx + NX - d, NX), h)
            pltpu.make_async_copy(there, there, out_recv.at[h, d - 1]).wait()

    over_heads(finish)


def local(queries, keys, values, block_picks, block_counts):
    picks = jnp.transpose(block_picks, (0, 2, 1))
    dma = pltpu.SemaphoreType.DMA
    return pl.pallas_call(
        kernel,
        out_shape=jax.ShapeDtypeStruct(queries.shape, queries.dtype),
        in_specs=[pl.BlockSpec(memory_space=pltpu.HBM)] * 5,
        out_specs=pl.BlockSpec(memory_space=pl.ANY),
        scratch_shapes=[
            pltpu.VMEM((SLOTS, HEADS, 2, ROWS, DIM), jnp.bfloat16),
            pltpu.VMEM((3,) + queries.shape, jnp.bfloat16),
            pltpu.VMEM((HEADS, ROWS, DIM), jnp.bfloat16),
            pltpu.VMEM((HEADS, ROWS, DIM), jnp.bfloat16),
            pltpu.VMEM((HEADS, DIM, ROWS), jnp.float32),
            pltpu.VMEM((HEADS, 1, ROWS), jnp.float32),
            pltpu.VMEM((HEADS, 8, ROWS), jnp.float32),
            pltpu.SMEM((1, GROUPS), jnp.int32),
            pltpu.SMEM((2, GROUPS), jnp.int32),
            dma((3, HEADS, 3)), dma((3, HEADS, 3)), dma((3, HEADS)),
            dma((SLOTS - M2, HEADS)), dma((SLOTS - M2, HEADS)),
            dma((2, 8, HEADS)), dma((2, 8, HEADS)), dma((2, 4, HEADS)), dma((2, 4, HEADS)),
            dma((HEADS, 3)), dma((HEADS, 3)), dma((HEADS,)), dma((5,)), pltpu.SemaphoreType.REGULAR((2,)),
        ],
        compiler_params=pltpu.CompilerParams(
            collective_id=0, has_side_effects=True, vmem_limit_bytes=32 * 1024 * 1024
        ),
        name="radial_attention",
    )(*(pltpu.with_memory_space_constraint(x, pltpu.HBM) for x in (queries, keys, values, picks, block_counts)))


def solution(mesh):
    placed = P(("frames", "heads"), None)
    return jax.shard_map(
        local,
        mesh=mesh,
        in_specs=(placed, placed, placed, P(), P()),
        out_specs=placed,
        check_vma=False,
    )
```

```python
import functools
import math

import jax
import jax.numpy as jnp
from jax import lax
from jax.experimental import pallas as pl
from jax.experimental.pallas import tpu as pltpu
from jax.sharding import PartitionSpec as P

MESH = pl.DeviceIdType.MESH

NZ, NY, NC, NX = 16, 4, 2, 4
GROUPS = NZ * NY * NC
HEADS = 3
DIM = 128
BLOCK = 128
TOK = 64
ROWS = TOK * NX
HIDE = 1e30
EXPONENT = math.log2(math.e) / math.sqrt(DIM)

OWN = 0
BELOW = 0
ABOVE = 8
M2, P2, M4, P4, SIB, SIB2, VIA_M4, VIA_P4 = 17, 18, 19, 20, 21, 22, 23, 24
SLOTS = 25

LONG = ((0, 1, 2, 3, 4, 6, 8), (0, 1, 2, 3, 4, 5, 6, 7, 8))
SHORT = ((0, 1, 2, 4), (0, 1, 2, 3, 4))

STAGES = (
    (
        ("long", 1), ("long", 2), ("long", 3), ("short", 1), ("long", 4), ("short", 2),
        ("long", 5), ("none", 0), ("short", 3), ("none", 0), ("long", 6), ("none", 0),
    ),
    (
        ("long", 1), ("long", 2), ("long", 3), ("short", 1), ("long", 4), ("long", 5),
        ("short", 2), ("long", 6), ("short", 3), ("long", 7), ("short", 4), ("long", 8),
    ),
)
COUNT = 12


def pick(index, values):
    found = values[-1]
    for i, value in enumerate(values[:-1]):
        found = jnp.where(index == i, value, found)
    return found


def kernel(
    q_hbm, k_hbm, v_hbm, picks_hbm, counts_hbm, out_hbm,
    kv, staged, qs, os, acc, top, total, counts, picks,
    in_send, in_recv, in_local, kv_send, kv_recv, long_send, long_recv, short_send, short_recv,
    out_send, out_recv, out_local, small_sem, entered,
):
    me = lax.axis_index("frames")
    mx = lax.axis_index("heads")
    core = lax.rem(me, NC)
    my = lax.rem(me // NC, NY)
    mz = me // (NC * NY)

    def frame(z, y, c):
        return (z * NY + y) * NC + c

    def along(way, chips):
        z = mz + chips if way == 0 else mz + NZ - chips
        return (frame(lax.rem(z, NZ), my, core), mx)

    right = (frame(mz, lax.rem(my + 1, NY), core), mx)
    left = (frame(mz, lax.rem(my + NY - 1, NY), core), mx)
    sibling = (frame(mz, my, 1 - core), mx)
    others = [(me, lax.rem(mx + d, NX)) for d in (1, 2, 3)]

    table = [
        pltpu.make_async_copy(counts_hbm.at[pl.ds(me, 1)], counts, small_sem.at[0]),
        pltpu.make_async_copy(picks_hbm.at[me], picks, small_sem.at[1]),
    ]
    staging = [
        pltpu.make_async_copy(source, staged.at[t], small_sem.at[2 + t])
        for t, source in enumerate((k_hbm, v_hbm, q_hbm))
    ]
    for copy in staging + table:
        copy.start()

    barrier = pltpu.get_barrier_semaphore()
    partners = [along(0, 1), along(1, 1), right, left, sibling] + others
    for partner in partners:
        pl.semaphore_signal(barrier, inc=1, device_id=partner, device_id_type=MESH)
    pl.semaphore_wait(barrier, len(partners))

    for way in (0, 1):
        pl.semaphore_signal(entered.at[way], inc=1, device_id=along(1 - way, 1), device_id_type=MESH)

    def landing(t, h, x):
        rows = pl.ds(pl.multiple_of(x * TOK, TOK), TOK)
        if t == 2:
            return qs.at[h, rows, :]
        return kv.at[OWN, h, t, rows, :]

    def piece(t, h, x):
        return staged.at[t, :, pl.ds(pl.multiple_of((x * HEADS + h) * DIM, DIM), DIM)]

    def exchange(t, h, d):
        target = lax.rem(mx + d, NX)
        return pltpu.make_async_remote_copy(
            src_ref=piece(t, h, target),
            dst_ref=landing(t, h, mx),
            send_sem=in_send.at[t, h, d - 1],
            recv_sem=in_recv.at[t, h, d - 1],
            device_id=(me, target),
            device_id_type=MESH,
        )

    def kept(t, h):
        return pltpu.make_async_copy(piece(t, h, mx), landing(t, h, mx), in_local.at[t, h])

    def arrived(t, h):
        kept(t, h).wait()
        for d in (1, 2, 3):
            source = lax.rem(mx + NX - d, NX)
            there = landing(t, h, source)
            pltpu.make_async_copy(there, there, in_recv.at[t, h, d - 1]).wait()

    def over_heads(body):
        def step(h, carry):
            body(h)
            return carry

        lax.fori_loop(0, HEADS, step, 0)

    def send_pieces(tensors, h):
        for t in tensors:
            for d in (2, 1, 3):
                exchange(t, h, d).start()
            kept(t, h).start()

    def pass_on(source, slot, h, target):
        return pltpu.make_async_remote_copy(
            src_ref=kv.at[source, h],
            dst_ref=kv.at[slot, h],
            send_sem=kv_send.at[slot - M2, h],
            recv_sem=kv_recv.at[slot - M2, h],
            device_id=target,
            device_id_type=MESH,
        )

    def await_slot(slot, h):
        there = kv.at[slot, h]
        pltpu.make_async_copy(there, there, kv_recv.at[slot - M2, h]).wait()

    depth = (mz, NZ - 1 - mz)

    def held(way, reach, h, t):
        return kv.at[jnp.where(reach == 0, OWN, (BELOW, ABOVE)[way] + reach), h, t]

    def by_core(zero, one):
        return jnp.where(core == 0, zero, one)

    def reach_of(s, reaches):
        return by_core(pick(s, reaches[0]), pick(s, reaches[1]))

    last_long, last_short = (by_core(len(r[0]) - 1, len(r[1]) - 1) for r in (LONG, SHORT))

    def pass_along(way, s, h, t, reaches, send, recv):
        start, end = reach_of(s - 1, reaches), reach_of(s, reaches)
        return pltpu.make_async_remote_copy(
            src_ref=held(way, start, h, t),
            dst_ref=held(way, end, h, t),
            send_sem=send.at[way, s - 1, h],
            recv_sem=recv.at[way, s - 1, h],
            device_id=along(way, end - start),
            device_id_type=MESH,
        )

    def pass_long(way, s, h):
        return pass_along(way, s, h, way, LONG, long_send, long_recv)

    def pass_short(way, s, h):
        return pass_along(way, s, h, 1 - way, SHORT, short_send, short_recv)

    def takes(way, s):
        d, reach = depth[way], reach_of(s, SHORT)
        return (s <= last_short) & (d >= reach) & ((reach != 3) | (d < NZ - 1))

    def gives(way, s):
        d, start, end = depth[way], reach_of(s - 1, SHORT), reach_of(s, SHORT)
        return (s <= last_short) & (d >= start) & (d < NZ - (end - start) - jnp.where(end == 3, 1, 0))

    def long_hop(s, h):
        for way in (0, 1):
            there = held(way, reach_of(s, LONG), h, way)
            pltpu.make_async_copy(there, there, long_recv.at[way, s - 1, h]).wait()

            @pl.when(s < last_long)
            def _():
                pass_long(way, s + 1, h).start()

    def short_hop(s, h):
        for way in (0, 1):
            @pl.when(takes(way, s))
            def _():
                there = held(way, reach_of(s, SHORT), h, 1 - way)
                pltpu.make_async_copy(there, there, short_recv.at[way, s - 1, h]).wait()

            @pl.when(gives(way, s + 1))
            def _():
                pass_short(way, s + 1, h).start()

    for way in (0, 1):
        for reach in (1, 2, 4):
            @pl.when(depth[way] < reach)
            def _():
                slot = (BELOW, ABOVE)[way] + reach
                for h in range(HEADS):
                    kv[slot, h, 1 - way] = jnp.zeros((ROWS, DIM), jnp.bfloat16)

    def first_hop(way, h, t, x, source):
        rows = pl.ds(pl.multiple_of(x * TOK, TOK), TOK)
        send, recv = (long_send, long_recv) if t == way else (short_send, short_recv)
        return pltpu.make_async_remote_copy(
            src_ref=source,
            dst_ref=held(way, 1, h, t).at[rows],
            send_sem=send.at[way, 0, h],
            recv_sem=recv.at[way, 0, h],
            device_id=along(way, 1),
            device_id_type=MESH,
        )

    def own_long(h):
        for way in (0, 1):
            first_hop(way, h, way, mx, piece(way, h, mx)).start()

    def own_short(h):
        for way in (0, 1):
            @pl.when(gives(way, 1))
            def _():
                first_hop(way, h, 1 - way, mx, piece(1 - way, h, mx)).start()

    def start_long(h):
        for d in (1, 3, 2):
            x = lax.rem(mx + NX - d, NX)
            for way in (0, 1):
                there = landing(way, h, x)
                pltpu.make_async_copy(there, there, in_recv.at[way, h, d - 1]).wait()
                first_hop(way, h, way, x, there).start()

    def start_short(h):
        for d in (1, 3, 2):
            x = lax.rem(mx + NX - d, NX)
            for way in (0, 1):
                @pl.when(gives(way, 1))
                def _():
                    first_hop(way, h, 1 - way, x, landing(1 - way, h, x)).start()

    staging[0].wait()
    staging[1].wait()
    send_pieces((0, 1), 0)
    over_heads(own_long)
    send_pieces((0, 1), 1)
    send_pieces((0, 1), 2)
    over_heads(own_short)
    over_heads(start_long)
    over_heads(start_short)
    staging[2].wait()
    over_heads(functools.partial(send_pieces, (2,)))

    def start_sibling(h):
        kept(0, h).wait()
        kept(1, h).wait()
        pass_on(OWN, SIB, h, sibling).start()

    over_heads(start_sibling)
    for way in (0, 1):
        pl.semaphore_wait(entered.at[way], 1)
    for copy in table:
        copy.wait()

    def bias_of(group):
        inside = (group >= 0) & (group < GROUPS)
        row = jnp.clip(group, 0, GROUPS - 1)
        count = jnp.where(inside, counts[0, row], 0)
        first, second = picks[0, row], picks[1, row]
        return [
            jnp.where(
                (group == me) | ((count > 0) & (first == j)) | ((count > 1) & (second == j)), 0.0, -HIDE
            )
            for j in (0, 1)
        ]

    def attend(h, parts):
        query = qs[h]
        raw, biases, highs = [], [], []
        for key_slot, _, group in parts:
            s = lax.dot_general(
                kv[key_slot, h, 0], query, (((1,), (1,)), ((), ())), preferred_element_type=jnp.float32
            )
            for j, bias in enumerate(bias_of(group)):
                block = s[j * BLOCK:(j + 1) * BLOCK]
                raw.append(block)
                biases.append(bias)
                highs.append(jnp.max(block, axis=0, keepdims=True) + bias)
        newest = functools.reduce(jnp.maximum, highs + [top[h]])
        rescale = jnp.exp2((top[h] - newest) * EXPONENT)
        row_sum = total[h] * rescale
        mixed = acc[h] * rescale
        for i, (_, value_slot, _) in enumerate(parts):
            weights = []
            for j in (2 * i, 2 * i + 1):
                w = jnp.exp2((raw[j] - (newest - biases[j])) * EXPONENT)
                weights.append(w.astype(jnp.bfloat16))
                row_sum = row_sum + jnp.sum(w.reshape(BLOCK // 8, 8, ROWS), axis=0)
            mixed = mixed + lax.dot_general(
                kv[value_slot, h, 1], jnp.concatenate(weights, axis=0),
                (((0,), (0,)), ((), ())), preferred_element_type=jnp.float32,
            )
        top[h] = newest
        total[h] = row_sum
        acc[h] = mixed

    top[...] = jnp.full(top.shape, -HIDE, jnp.float32)
    total[...] = jnp.zeros(total.shape, jnp.float32)
    acc[...] = jnp.zeros(acc.shape, jnp.float32)

    zstep = NY * NC
    own_pair = ((OWN, OWN, me), (SIB, SIB, me + 1 - 2 * core))
    far = lax.rem(me + 8 * zstep, GROUPS)
    sib2 = (SIB2, SIB2, me - 1 + 2 * core)
    opposite = (BELOW + 8, ABOVE + 8, far)

    def near(k):
        return (
            (BELOW + k, BELOW + k, me - k * zstep),
            (ABOVE + k, ABOVE + k, me + k * zstep),
        )

    two_pair = ((M2, M2, me - 2), (P2, P2, me + 2))
    four_pair = ((M4, M4, me - 4), (P4, P4, me + 4))
    pairs = [
        (by_core(*at), pair) for at, pair in (
            ((0, 0), own_pair), ((3, 4), near(1)), ((5, 6), two_pair),
            ((6, 7), near(2)), ((7, 9), four_pair), ((8, 10), near(4)),
        )
    ]
    far_stage = by_core(10, 11)

    def chosen(stage, side):
        found = own_pair[side]
        for at, pair in pairs[1:]:
            found = tuple(jnp.where(stage == at, new, old) for new, old in zip(pair[side], found))
        return found

    def extras(stage, h):
        @pl.when(stage == 0)
        def _():
            arrived(2, h)
            await_slot(SIB, h)

        @pl.when(((stage == 0) & (my < NY - 1)) | ((stage == 3) & (my == NY - 1)))
        def _():
            pass_on(jnp.where(my == NY - 1, BELOW + 1, OWN), M2, h, right).start()

        @pl.when(((stage == 1) & (my > 0)) | ((stage == 3) & (my == 0)))
        def _():
            pass_on(jnp.where(my == 0, ABOVE + 1, OWN), P2, h, left).start()

        @pl.when((stage == 3) & (my == 2))
        def _():
            pass_on(BELOW + 1, VIA_M4, h, right).start()

        @pl.when((stage == 3) & (my == 1))
        def _():
            pass_on(ABOVE + 1, VIA_P4, h, left).start()

        @pl.when(stage == by_core(5, 6))
        def _():
            await_slot(M2, h)
            await_slot(P2, h)
            pass_on(jnp.where(core == 1, M2, P2), SIB2, h, sibling).start()

            @pl.when(my == NY - 1)
            def _():
                await_slot(VIA_M4, h)

            @pl.when(my == 0)
            def _():
                await_slot(VIA_P4, h)

            pass_on(jnp.where(my == NY - 1, VIA_M4, M2), M4, h, right).start()
            pass_on(jnp.where(my == 0, VIA_P4, P2), P4, h, left).start()

        @pl.when(stage == 8)
        def _():
            await_slot(SIB2, h)
            for t in (0, 1, 2):
                for d in (1, 2, 3):
                    exchange(t, h, d).wait_send()
            release(h, (SIB, M2, P2), (1, 2, 3), (1, 2))
            for slot, place in ((VIA_M4, 2), (VIA_P4, 1)):
                @pl.when(my == place)
                def _():
                    pass_on(OWN, slot, h, sibling).wait_send()

        @pl.when(stage == by_core(7, 9))
        def _():
            await_slot(M4, h)
            await_slot(P4, h)


    def release(h, slots, long_hops, short_hops):
        for slot in slots:
            pass_on(OWN, slot, h, sibling).wait_send()
        for way in (0, 1):
            for k in long_hops:
                @pl.when(k <= last_long)
                def _():
                    pass_long(way, k, h).wait_send()

            for k in short_hops:
                @pl.when(gives(way, k))
                def _():
                    pass_short(way, k, h).wait_send()

    def one_stage(stage, carry):
        def is_kind(name):
            return by_core(*(
                functools.reduce(
                    jnp.logical_or, [stage == i for i, (kind, _) in enumerate(stages) if kind == name]
                )
                for stages in STAGES
            ))

        hop = by_core(*(pick(stage, [s for _, s in stages]) for stages in STAGES))
        is_long, is_short = is_kind("long"), is_kind("short")
        attends = functools.reduce(jnp.logical_or, [stage == at for at, _ in pairs])
        first, second = chosen(stage, 0), chosen(stage, 1)
        alone = (stage == 8) | (stage == far_stage)
        single = tuple(jnp.where(stage == 8, *entry) for entry in zip(sib2, opposite))

        def one_head(h):
            @pl.when(is_long)
            def _():
                long_hop(hop, h)

            @pl.when(is_short)
            def _():
                short_hop(hop, h)

            extras(stage, h)

            @pl.when(attends)
            def _():
                attend(h, [first, second])

            @pl.when(alone)
            def _():
                attend(h, [single])

            @pl.when(stage == far_stage)
            def _():
                finish_head(h)

        over_heads(one_head)
        return carry

    def out_columns(x, h):
        return out_hbm.at[:, pl.ds(pl.multiple_of((x * HEADS + h) * DIM, DIM), DIM)]

    def out_rows(x, h):
        return os.at[h, pl.ds(pl.multiple_of(x * TOK, TOK), TOK), :]

    def give_back(h, d):
        target = lax.rem(mx + d, NX)
        return pltpu.make_async_remote_copy(
            src_ref=out_rows(target, h),
            dst_ref=out_columns(mx, h),
            send_sem=out_send.at[h, d - 1],
            recv_sem=out_recv.at[h, d - 1],
            device_id=(me, target),
            device_id_type=MESH,
        )

    def keep_back(h):
        return pltpu.make_async_copy(out_rows(mx, h), out_columns(mx, h), out_local.at[h])

    def finish_head(h):
        row_total = jnp.sum(total[h], axis=0, keepdims=True)
        os[h] = jnp.transpose(acc[h] / row_total).astype(jnp.bfloat16)
        for d in (2, 1, 3):
            give_back(h, d).start()
        keep_back(h).start()

    lax.fori_loop(0, COUNT, one_stage, 0)

    def finish(h):
        release(h, (M4, P4, SIB2), (4, 5, 6, 7, 8), (3, 4))
        for d in (1, 2, 3):
            give_back(h, d).wait_send()
        keep_back(h).wait()
        for d in (1, 2, 3):
            there = out_columns(lax.rem(mx + NX - d, NX), h)
            pltpu.make_async_copy(there, there, out_recv.at[h, d - 1]).wait()

    over_heads(finish)


def local(queries, keys, values, block_picks, block_counts):
    picks = jnp.transpose(block_picks, (0, 2, 1))
    dma = pltpu.SemaphoreType.DMA
    return pl.pallas_call(
        kernel,
        out_shape=jax.ShapeDtypeStruct(queries.shape, queries.dtype),
        in_specs=[pl.BlockSpec(memory_space=pltpu.HBM)] * 5,
        out_specs=pl.BlockSpec(memory_space=pl.ANY),
        scratch_shapes=[
            pltpu.VMEM((SLOTS, HEADS, 2, ROWS, DIM), jnp.bfloat16),
            pltpu.VMEM((3,) + queries.shape, jnp.bfloat16),
            pltpu.VMEM((HEADS, ROWS, DIM), jnp.bfloat16),
            pltpu.VMEM((HEADS, ROWS, DIM), jnp.bfloat16),
            pltpu.VMEM((HEADS, DIM, ROWS), jnp.float32),
            pltpu.VMEM((HEADS, 1, ROWS), jnp.float32),
            pltpu.VMEM((HEADS, 8, ROWS), jnp.float32),
            pltpu.SMEM((1, GROUPS), jnp.int32),
            pltpu.SMEM((2, GROUPS), jnp.int32),
            dma((3, HEADS, 3)), dma((3, HEADS, 3)), dma((3, HEADS)),
            dma((SLOTS - M2, HEADS)), dma((SLOTS - M2, HEADS)),
            dma((2, 8, HEADS)), dma((2, 8, HEADS)), dma((2, 4, HEADS)), dma((2, 4, HEADS)),
            dma((HEADS, 3)), dma((HEADS, 3)), dma((HEADS,)), dma((5,)), pltpu.SemaphoreType.REGULAR((2,)),
        ],
        compiler_params=pltpu.CompilerParams(
            collective_id=0, has_side_effects=True, vmem_limit_bytes=32 * 1024 * 1024
        ),
        name="radial_attention",
    )(*(pltpu.with_memory_space_constraint(x, pltpu.HBM) for x in (queries, keys, values, picks, block_counts)))


def solution(mesh):
    placed = P(("frames", "heads"), None)
    return jax.shard_map(
        local,
        mesh=mesh,
        in_specs=(placed, placed, placed, P(), P()),
        out_specs=placed,
        check_vma=False,
    )
```

```python
import functools
import math

import jax
import jax.numpy as jnp
from jax import lax
from jax.experimental import pallas as pl
from jax.experimental.pallas import tpu as pltpu
from jax.sharding import PartitionSpec as P

MESH = pl.DeviceIdType.MESH

NZ, NY, NC, NX = 16, 4, 2, 4
GROUPS = NZ * NY * NC
HEADS = 3
DIM = 128
BLOCK = 128
TOK = 64
ROWS = TOK * NX
HIDE = 1e30
EXPONENT = math.log2(math.e) / math.sqrt(DIM)

OWN = 0
BELOW = 0
ABOVE = 8
M2, P2, M4, P4, SIB, SIB2, VIA_M4, VIA_P4 = 17, 18, 19, 20, 21, 22, 23, 24
SLOTS = 25

LONG = ((0, 1, 2, 4, 6, 8), (0, 1, 2, 3, 4, 5, 6, 8))
SHORT = ((0, 1, 2, 4), (0, 1, 2, 3, 4))

STAGES = (
    (
        ("long", 1), ("long", 2), ("short", 1), ("long", 3), ("short", 2), ("long", 4),
        ("none", 0), ("short", 3), ("none", 0), ("long", 5), ("none", 0), ("none", 0),
    ),
    (
        ("long", 1), ("long", 2), ("long", 3), ("short", 1), ("long", 4), ("long", 5),
        ("short", 2), ("long", 6), ("short", 3), ("none", 0), ("short", 4), ("long", 7),
    ),
)
COUNT = 12


def pick(index, values):
    found = values[-1]
    for i, value in enumerate(values[:-1]):
        found = jnp.where(index == i, value, found)
    return found


def kernel(
    q_hbm, k_hbm, v_hbm, picks_hbm, counts_hbm, out_hbm,
    kv, staged, qs, os, acc, top, total, counts, picks,
    in_send, in_recv, in_local, kv_send, kv_recv, long_send, long_recv, short_send, short_recv,
    out_send, out_recv, out_local, small_sem, entered,
):
    me = lax.axis_index("frames")
    mx = lax.axis_index("heads")
    core = lax.rem(me, NC)
    my = lax.rem(me // NC, NY)
    mz = me // (NC * NY)

    def frame(z, y, c):
        return (z * NY + y) * NC + c

    def along(way, chips):
        z = mz + chips if way == 0 else mz + NZ - chips
        return (frame(lax.rem(z, NZ), my, core), mx)

    right = (frame(mz, lax.rem(my + 1, NY), core), mx)
    left = (frame(mz, lax.rem(my + NY - 1, NY), core), mx)
    sibling = (frame(mz, my, 1 - core), mx)
    others = [(me, lax.rem(mx + d, NX)) for d in (1, 2, 3)]

    table = [
        pltpu.make_async_copy(counts_hbm.at[pl.ds(me, 1)], counts, small_sem.at[0]),
        pltpu.make_async_copy(picks_hbm.at[me], picks, small_sem.at[1]),
    ]
    staging = [
        pltpu.make_async_copy(source, staged.at[t], small_sem.at[2 + t])
        for t, source in enumerate((k_hbm, v_hbm, q_hbm))
    ]
    for copy in staging + table:
        copy.start()

    barrier = pltpu.get_barrier_semaphore()
    partners = [along(0, 1), along(1, 1), right, left, sibling] + others
    for partner in partners:
        pl.semaphore_signal(barrier, inc=1, device_id=partner, device_id_type=MESH)
    pl.semaphore_wait(barrier, len(partners))

    for way in (0, 1):
        pl.semaphore_signal(entered.at[way], inc=1, device_id=along(1 - way, 1), device_id_type=MESH)

    def landing(t, h, x):
        rows = pl.ds(pl.multiple_of(x * TOK, TOK), TOK)
        if t == 2:
            return qs.at[h, rows, :]
        return kv.at[OWN, h, t, rows, :]

    def piece(t, h, x):
        return staged.at[t, :, pl.ds(pl.multiple_of((x * HEADS + h) * DIM, DIM), DIM)]

    def exchange(t, h, d):
        target = lax.rem(mx + d, NX)
        return pltpu.make_async_remote_copy(
            src_ref=piece(t, h, target),
            dst_ref=landing(t, h, mx),
            send_sem=in_send.at[t, h, d - 1],
            recv_sem=in_recv.at[t, h, d - 1],
            device_id=(me, target),
            device_id_type=MESH,
        )

    def kept(t, h):
        return pltpu.make_async_copy(piece(t, h, mx), landing(t, h, mx), in_local.at[t, h])

    def arrived(t, h):
        kept(t, h).wait()
        for d in (1, 2, 3):
            source = lax.rem(mx + NX - d, NX)
            there = landing(t, h, source)
            pltpu.make_async_copy(there, there, in_recv.at[t, h, d - 1]).wait()

    def over_heads(body):
        def step(h, carry):
            body(h)
            return carry

        lax.fori_loop(0, HEADS, step, 0)

    def send_pieces(tensors, h):
        for t in tensors:
            for d in (2, 1, 3):
                exchange(t, h, d).start()
            kept(t, h).start()

    def pass_on(source, slot, h, target):
        return pltpu.make_async_remote_copy(
            src_ref=kv.at[source, h],
            dst_ref=kv.at[slot, h],
            send_sem=kv_send.at[slot - M2, h],
            recv_sem=kv_recv.at[slot - M2, h],
            device_id=target,
            device_id_type=MESH,
        )

    def await_slot(slot, h):
        there = kv.at[slot, h]
        pltpu.make_async_copy(there, there, kv_recv.at[slot - M2, h]).wait()

    depth = (mz, NZ - 1 - mz)

    def held(way, reach, h, t):
        return kv.at[jnp.where(reach == 0, OWN, (BELOW, ABOVE)[way] + reach), h, t]

    def by_core(zero, one):
        return jnp.where(core == 0, zero, one)

    def reach_of(s, reaches):
        return by_core(pick(s, reaches[0]), pick(s, reaches[1]))

    last_long, last_short = (by_core(len(r[0]) - 1, len(r[1]) - 1) for r in (LONG, SHORT))

    def pass_along(way, s, h, t, reaches, send, recv):
        start, end = reach_of(s - 1, reaches), reach_of(s, reaches)
        return pltpu.make_async_remote_copy(
            src_ref=held(way, start, h, t),
            dst_ref=held(way, end, h, t),
            send_sem=send.at[way, s - 1, h],
            recv_sem=recv.at[way, s - 1, h],
            device_id=along(way, end - start),
            device_id_type=MESH,
        )

    def pass_long(way, s, h):
        return pass_along(way, s, h, way, LONG, long_send, long_recv)

    def pass_short(way, s, h):
        return pass_along(way, s, h, 1 - way, SHORT, short_send, short_recv)

    def takes(way, s):
        d, reach = depth[way], reach_of(s, SHORT)
        return (s <= last_short) & (d >= reach) & ((reach != 3) | (d < NZ - 1))

    def gives(way, s):
        d, start, end = depth[way], reach_of(s - 1, SHORT), reach_of(s, SHORT)
        return (s <= last_short) & (d >= start) & (d < NZ - (end - start) - jnp.where(end == 3, 1, 0))

    def long_hop(s, h):
        for way in (0, 1):
            there = held(way, reach_of(s, LONG), h, way)
            pltpu.make_async_copy(there, there, long_recv.at[way, s - 1, h]).wait()

            @pl.when(s < last_long)
            def _():
                pass_long(way, s + 1, h).start()

    def short_hop(s, h):
        for way in (0, 1):
            @pl.when(takes(way, s))
            def _():
                there = held(way, reach_of(s, SHORT), h, 1 - way)
                pltpu.make_async_copy(there, there, short_recv.at[way, s - 1, h]).wait()

            @pl.when(gives(way, s + 1))
            def _():
                pass_short(way, s + 1, h).start()

    for way in (0, 1):
        for reach in (1, 2, 4):
            @pl.when(depth[way] < reach)
            def _():
                slot = (BELOW, ABOVE)[way] + reach
                for h in range(HEADS):
                    kv[slot, h, 1 - way] = jnp.zeros((ROWS, DIM), jnp.bfloat16)

    def first_hop(way, h, t, x, source):
        rows = pl.ds(pl.multiple_of(x * TOK, TOK), TOK)
        send, recv = (long_send, long_recv) if t == way else (short_send, short_recv)
        return pltpu.make_async_remote_copy(
            src_ref=source,
            dst_ref=held(way, 1, h, t).at[rows],
            send_sem=send.at[way, 0, h],
            recv_sem=recv.at[way, 0, h],
            device_id=along(way, 1),
            device_id_type=MESH,
        )

    def own_long(h):
        for way in (0, 1):
            first_hop(way, h, way, mx, piece(way, h, mx)).start()

    def own_short(h):
        for way in (0, 1):
            @pl.when(gives(way, 1))
            def _():
                first_hop(way, h, 1 - way, mx, piece(1 - way, h, mx)).start()

    def start_long(h):
        for d in (1, 3, 2):
            x = lax.rem(mx + NX - d, NX)
            for way in (0, 1):
                there = landing(way, h, x)
                pltpu.make_async_copy(there, there, in_recv.at[way, h, d - 1]).wait()
                first_hop(way, h, way, x, there).start()

    def start_short(h):
        for d in (1, 3, 2):
            x = lax.rem(mx + NX - d, NX)
            for way in (0, 1):
                @pl.when(gives(way, 1))
                def _():
                    first_hop(way, h, 1 - way, x, landing(1 - way, h, x)).start()

    staging[0].wait()
    staging[1].wait()
    send_pieces((0, 1), 0)
    over_heads(own_long)
    send_pieces((0, 1), 1)
    send_pieces((0, 1), 2)
    over_heads(own_short)
    over_heads(start_long)
    over_heads(start_short)
    staging[2].wait()
    over_heads(functools.partial(send_pieces, (2,)))

    def start_sibling(h):
        kept(0, h).wait()
        kept(1, h).wait()
        pass_on(OWN, SIB, h, sibling).start()

    over_heads(start_sibling)
    for way in (0, 1):
        pl.semaphore_wait(entered.at[way], 1)
    for copy in table:
        copy.wait()

    def bias_of(group):
        inside = (group >= 0) & (group < GROUPS)
        row = jnp.clip(group, 0, GROUPS - 1)
        count = jnp.where(inside, counts[0, row], 0)
        first, second = picks[0, row], picks[1, row]
        return [
            jnp.where(
                (group == me) | ((count > 0) & (first == j)) | ((count > 1) & (second == j)), 0.0, -HIDE
            )
            for j in (0, 1)
        ]

    def attend(h, parts):
        query = qs[h]
        raw, biases, highs = [], [], []
        for key_slot, _, group in parts:
            s = lax.dot_general(
                kv[key_slot, h, 0], query, (((1,), (1,)), ((), ())), preferred_element_type=jnp.float32
            )
            for j, bias in enumerate(bias_of(group)):
                block = s[j * BLOCK:(j + 1) * BLOCK]
                raw.append(block)
                biases.append(bias)
                highs.append(jnp.max(block, axis=0, keepdims=True) + bias)
        newest = functools.reduce(jnp.maximum, highs + [top[h]])
        rescale = jnp.exp2((top[h] - newest) * EXPONENT)
        row_sum = total[h] * rescale
        mixed = acc[h] * rescale
        for i, (_, value_slot, _) in enumerate(parts):
            weights = []
            for j in (2 * i, 2 * i + 1):
                w = jnp.exp2((raw[j] - (newest - biases[j])) * EXPONENT)
                weights.append(w.astype(jnp.bfloat16))
                row_sum = row_sum + jnp.sum(w.reshape(BLOCK // 8, 8, ROWS), axis=0)
            mixed = mixed + lax.dot_general(
                kv[value_slot, h, 1], jnp.concatenate(weights, axis=0),
                (((0,), (0,)), ((), ())), preferred_element_type=jnp.float32,
            )
        top[h] = newest
        total[h] = row_sum
        acc[h] = mixed

    top[...] = jnp.full(top.shape, -HIDE, jnp.float32)
    total[...] = jnp.zeros(total.shape, jnp.float32)
    acc[...] = jnp.zeros(acc.shape, jnp.float32)

    zstep = NY * NC
    own_pair = ((OWN, OWN, me), (SIB, SIB, me + 1 - 2 * core))
    far = lax.rem(me + 8 * zstep, GROUPS)
    sib2 = (SIB2, SIB2, me - 1 + 2 * core)
    opposite = (BELOW + 8, ABOVE + 8, far)

    def near(k):
        return (
            (BELOW + k, BELOW + k, me - k * zstep),
            (ABOVE + k, ABOVE + k, me + k * zstep),
        )

    two_pair = ((M2, M2, me - 2), (P2, P2, me + 2))
    four_pair = ((M4, M4, me - 4), (P4, P4, me + 4))
    pairs = [
        (by_core(*at), pair) for at, pair in (
            ((0, 0), own_pair), ((2, 4), near(1)), ((4, 6), two_pair),
            ((5, 7), near(2)), ((6, 9), four_pair), ((7, 10), near(4)),
        )
    ]
    far_stage = by_core(9, 11)

    def chosen(stage, side):
        found = own_pair[side]
        for at, pair in pairs[1:]:
            found = tuple(jnp.where(stage == at, new, old) for new, old in zip(pair[side], found))
        return found

    def extras(stage, h):
        @pl.when(stage == 0)
        def _():
            arrived(2, h)
            await_slot(SIB, h)

        @pl.when(((stage == 0) & (my < NY - 1)) | ((stage == by_core(2, 3)) & (my == NY - 1)))
        def _():
            pass_on(jnp.where(my == NY - 1, BELOW + 1, OWN), M2, h, right).start()

        @pl.when(((stage == 1) & (my > 0)) | ((stage == by_core(2, 3)) & (my == 0)))
        def _():
            pass_on(jnp.where(my == 0, ABOVE + 1, OWN), P2, h, left).start()

        @pl.when((stage == by_core(2, 3)) & (my == 2))
        def _():
            pass_on(BELOW + 1, VIA_M4, h, right).start()

        @pl.when((stage == by_core(2, 3)) & (my == 1))
        def _():
            pass_on(ABOVE + 1, VIA_P4, h, left).start()

        @pl.when(stage == by_core(4, 6))
        def _():
            await_slot(M2, h)
            await_slot(P2, h)
            pass_on(jnp.where(core == 1, M2, P2), SIB2, h, sibling).start()

            @pl.when(my == NY - 1)
            def _():
                await_slot(VIA_M4, h)

            @pl.when(my == 0)
            def _():
                await_slot(VIA_P4, h)

            pass_on(jnp.where(my == NY - 1, VIA_M4, M2), M4, h, right).start()
            pass_on(jnp.where(my == 0, VIA_P4, P2), P4, h, left).start()

        @pl.when(stage == 8)
        def _():
            await_slot(SIB2, h)
            for t in (0, 1, 2):
                for d in (1, 2, 3):
                    exchange(t, h, d).wait_send()
            release(h, (SIB, M2, P2), (1, 2, 3), (1, 2))
            for slot, place in ((VIA_M4, 2), (VIA_P4, 1)):
                @pl.when(my == place)
                def _():
                    pass_on(OWN, slot, h, sibling).wait_send()

        @pl.when(stage == by_core(6, 9))
        def _():
            await_slot(M4, h)
            await_slot(P4, h)


    def release(h, slots, long_hops, short_hops):
        for slot in slots:
            pass_on(OWN, slot, h, sibling).wait_send()
        for way in (0, 1):
            for k in long_hops:
                @pl.when(k <= last_long)
                def _():
                    pass_long(way, k, h).wait_send()

            for k in short_hops:
                @pl.when(gives(way, k))
                def _():
                    pass_short(way, k, h).wait_send()

    def one_stage(stage, carry):
        def is_kind(name):
            return by_core(*(
                functools.reduce(
                    jnp.logical_or, [stage == i for i, (kind, _) in enumerate(stages) if kind == name]
                )
                for stages in STAGES
            ))

        hop = by_core(*(pick(stage, [s for _, s in stages]) for stages in STAGES))
        is_long, is_short = is_kind("long"), is_kind("short")
        attends = functools.reduce(jnp.logical_or, [stage == at for at, _ in pairs])
        first, second = chosen(stage, 0), chosen(stage, 1)
        alone = (stage == 8) | (stage == far_stage)
        single = tuple(jnp.where(stage == 8, *entry) for entry in zip(sib2, opposite))

        def one_head(h):
            @pl.when(is_long)
            def _():
                long_hop(hop, h)

            @pl.when(is_short)
            def _():
                short_hop(hop, h)

            extras(stage, h)

            @pl.when(attends)
            def _():
                attend(h, [first, second])

            @pl.when(alone)
            def _():
                attend(h, [single])

            @pl.when(stage == far_stage)
            def _():
                finish_head(h)

        over_heads(one_head)
        return carry

    def out_columns(x, h):
        return out_hbm.at[:, pl.ds(pl.multiple_of((x * HEADS + h) * DIM, DIM), DIM)]

    def out_rows(x, h):
        return os.at[h, pl.ds(pl.multiple_of(x * TOK, TOK), TOK), :]

    def give_back(h, d):
        target = lax.rem(mx + d, NX)
        return pltpu.make_async_remote_copy(
            src_ref=out_rows(target, h),
            dst_ref=out_columns(mx, h),
            send_sem=out_send.at[h, d - 1],
            recv_sem=out_recv.at[h, d - 1],
            device_id=(me, target),
            device_id_type=MESH,
        )

    def keep_back(h):
        return pltpu.make_async_copy(out_rows(mx, h), out_columns(mx, h), out_local.at[h])

    def finish_head(h):
        row_total = jnp.sum(total[h], axis=0, keepdims=True)
        os[h] = jnp.transpose(acc[h] / row_total).astype(jnp.bfloat16)
        for d in (2, 1, 3):
            give_back(h, d).start()
        keep_back(h).start()

    lax.fori_loop(0, COUNT, one_stage, 0)

    def finish(h):
        release(h, (M4, P4, SIB2), (4, 5, 6, 7, 8), (3, 4))
        for d in (1, 2, 3):
            give_back(h, d).wait_send()
        keep_back(h).wait()
        for d in (1, 2, 3):
            there = out_columns(lax.rem(mx + NX - d, NX), h)
            pltpu.make_async_copy(there, there, out_recv.at[h, d - 1]).wait()

    over_heads(finish)


def local(queries, keys, values, block_picks, block_counts):
    picks = jnp.transpose(block_picks, (0, 2, 1))
    dma = pltpu.SemaphoreType.DMA
    return pl.pallas_call(
        kernel,
        out_shape=jax.ShapeDtypeStruct(queries.shape, queries.dtype),
        in_specs=[pl.BlockSpec(memory_space=pltpu.HBM)] * 5,
        out_specs=pl.BlockSpec(memory_space=pl.ANY),
        scratch_shapes=[
            pltpu.VMEM((SLOTS, HEADS, 2, ROWS, DIM), jnp.bfloat16),
            pltpu.VMEM((3,) + queries.shape, jnp.bfloat16),
            pltpu.VMEM((HEADS, ROWS, DIM), jnp.bfloat16),
            pltpu.VMEM((HEADS, ROWS, DIM), jnp.bfloat16),
            pltpu.VMEM((HEADS, DIM, ROWS), jnp.float32),
            pltpu.VMEM((HEADS, 1, ROWS), jnp.float32),
            pltpu.VMEM((HEADS, 8, ROWS), jnp.float32),
            pltpu.SMEM((1, GROUPS), jnp.int32),
            pltpu.SMEM((2, GROUPS), jnp.int32),
            dma((3, HEADS, 3)), dma((3, HEADS, 3)), dma((3, HEADS)),
            dma((SLOTS - M2, HEADS)), dma((SLOTS - M2, HEADS)),
            dma((2, 8, HEADS)), dma((2, 8, HEADS)), dma((2, 4, HEADS)), dma((2, 4, HEADS)),
            dma((HEADS, 3)), dma((HEADS, 3)), dma((HEADS,)), dma((5,)), pltpu.SemaphoreType.REGULAR((2,)),
        ],
        compiler_params=pltpu.CompilerParams(
            collective_id=0, has_side_effects=True, vmem_limit_bytes=32 * 1024 * 1024
        ),
        name="radial_attention",
    )(*(pltpu.with_memory_space_constraint(x, pltpu.HBM) for x in (queries, keys, values, picks, block_counts)))


def solution(mesh):
    placed = P(("frames", "heads"), None)
    return jax.shard_map(
        local,
        mesh=mesh,
        in_specs=(placed, placed, placed, P(), P()),
        out_specs=placed,
        check_vma=False,
    )
```
